256 devices in a mesh: freq: 8 (over z), row: 4 (over x), col: 8 (over y, core).
Axes of the slice: x: 4, y: 4, z: 8, core: 2. Of those that a mesh axis runs over, the one named last changes fastest.
Arguments:
- prior_factor: bfloat16 [8, 26624, 1024], P('freq', ('row', 'col')), may hold values from -1 to 1, as said below
- prior_seeds: int32 [8, 26624, 512], P('freq', ('row', 'col')), may hold values from 0 to 4095
- window_seeds: int32 [8, 1024, 512], P('freq'), may hold values from 0 to 4095
- spectra: float32 [8, 1024], P('freq'), may hold values from 0.25 to 1
- nugget: float32 [8, 1024], P('freq'), may hold values from 0.6 to 1.2
- decay: float32 [8], P('freq'), may hold values from 0.2 to 2
Outputs:
- velocity: float32 [512, 1024, 256], P('freq', ('row', 'col'))
The draws below stay inside these ranges and needn't reach their ends.
Inputs may be any that keep to these rules, and one draw needn't show every extreme that they name: `prior_factor`: every entry is smaller in magnitude than 0.95 / (sqrt(26624) + sqrt(1024)), and window_matrix is positive definite.
All inputs are finite; a program needn't handle non-finite values.
Results may differ from the reference program's by a relative error of at most 0.00087.
Values sent between devices are 32-bit elements; how exact they have to be, the bound alone decides.
No kernel may reach another device: no remote copies, remote signals or barrier semaphores. Data moves between devices by JAX's collectives and lax.ppermute only.
A program may use at most 128 MiB of HBM per device.

```python
import math
import jax
import jax.numpy as jnp
from jax import lax

GRID = 96
NPHASE = 4096
SEEDS = 512
STEPS = 256
WINDOW = 1024
PRIOR = 26624
FREQS = 8
FIRST_BIN = 64
N_ROW = 4
N_COL = 8


def draw_prior_factor(key, part):
    limit = math.sqrt(0.9) / (math.sqrt(PRIOR) + math.sqrt(WINDOW))
    values = jax.random.uniform(key, (FREQS, PRIOR, WINDOW), jnp.float32, -limit, limit)
    return values.astype(jnp.bfloat16)


def plant(result, stream_key, smallest, high):
    dims = result.shape
    spot = [jax.random.randint(jax.random.fold_in(stream_key, axis), (), 0, dims[axis]) for axis in range(len(dims))]
    result = result.at[tuple(spot)].set(smallest)
    longest = dims.index(max(dims))
    spot[longest] = (spot[longest] + 1) % dims[longest]
    return result.at[tuple(spot)].set(high)


def steps_of(rng, dims, split, least, high):
    def one(axis_at, blocks):
        steps = jax.random.uniform(jax.random.fold_in(jax.random.fold_in(rng, 6), axis_at), (blocks,), jnp.float32, least / len(split), high / len(split))
        return jnp.repeat(jnp.exp(steps), dims[axis_at] // blocks).reshape((-1,) + (1,) * (len(dims) - axis_at - 1))

    gain = one(*split[0])
    for cut in split[1:]:
        gain = gain * one(*cut)
    return gain


def setup_inputs(seed: int = 0) -> dict:
    arg_keys = jax.random.split(jax.random.key(seed), 7)
    return {
        "prior_factor": draw_prior_factor(jax.random.fold_in(arg_keys[6], 71), 0),
        "prior_seeds": plant(jax.random.randint(arg_keys[1], (FREQS, PRIOR, SEEDS), 0, NPHASE), jax.random.fold_in(arg_keys[1], 1), 0, NPHASE - 1).astype(jnp.int32),
        "window_seeds": plant(jax.random.randint(arg_keys[2], (FREQS, WINDOW, SEEDS), 0, NPHASE), jax.random.fold_in(arg_keys[2], 1), 0, NPHASE - 1).astype(jnp.int32),
        "spectra": jnp.clip(jnp.exp(math.log(1.0) - 1.3862944 * jax.random.uniform(arg_keys[3], (FREQS, WINDOW), jnp.float32) ** steps_of(arg_keys[3], (FREQS, WINDOW), ((0, 8),), -0.2, 0.2)), 0.25, 1.0),
        "nugget": jnp.clip(0.6 + 0.6 * jax.random.uniform(arg_keys[4], (FREQS, WINDOW), jnp.float32) ** steps_of(arg_keys[4], (FREQS, WINDOW), ((0, 8),), -0.2, 0.2), 0.6, 1.2),
        "decay": jnp.clip(jnp.exp(math.log(2.0) - 2.3025851 * jax.random.uniform(arg_keys[5], (FREQS,), jnp.float32) ** steps_of(arg_keys[5], (FREQS,), ((0, 8),), -0.2, 0.2)), 0.2, 2.0),
    }


cross_weight = 0.3

def window_index(positions, window, parts):
    own = window // parts
    quarter = own // 2
    device = positions // own
    within = positions % own
    return jnp.where(within < quarter, device * quarter + within, window // 2 + device * quarter + within - quarter).astype(jnp.int32)

def coherence(spectra, nugget, decay, row_ids):
    window = spectra.shape[0]
    col_ids = jnp.arange(window, dtype=jnp.int32)
    row_global = PRIOR + row_ids
    col_global = PRIOR + col_ids
    row_points = row_global // 3
    col_points = col_global // 3
    row_across = (row_points % GRID).astype(jnp.float32)
    row_height = (row_points // GRID).astype(jnp.float32)
    col_across = (col_points % GRID).astype(jnp.float32)
    col_height = (col_points // GRID).astype(jnp.float32)
    distance = jnp.sqrt((row_across[:, None] - col_across[None, :]) ** 2 + (row_height[:, None] - col_height[None, :]) ** 2)
    coupling = jnp.where((row_global % 3)[:, None] == (col_global % 3)[None, :], jnp.float32(1.0), jnp.float32(cross_weight))
    row_spectra = jnp.take(spectra, row_ids)
    row_nugget = jnp.take(nugget, row_ids)
    amplitude = jnp.sqrt(row_spectra[:, None] * spectra[None, :])
    diagonal = jnp.where(row_ids[:, None] == col_ids[None, :], row_nugget[:, None], jnp.float32(0.0))
    return coupling * amplitude * jnp.exp(-decay * distance) + diagonal

def reference(prior_factor, prior_seeds, window_seeds, spectra, nugget, decay):
    re_parts = []
    im_parts = []
    natural_ids = jnp.arange(WINDOW, dtype=jnp.int32)
    for freq_index in range(FREQS):
        prior_cols = prior_factor[freq_index]
        schur = jnp.dot(prior_cols.T.astype(jnp.float32), prior_cols.astype(jnp.float32), preferred_element_type=jnp.float32)
        window_matrix = coherence(spectra[freq_index], nugget[freq_index], decay[freq_index], natural_ids) - schur
        factor = jnp.linalg.cholesky(window_matrix)
        phases = 2.0 * math.pi / NPHASE * prior_seeds[freq_index].astype(jnp.float32)
        wave_re = jnp.cos(phases).astype(jnp.bfloat16)
        wave_im = jnp.sin(phases).astype(jnp.bfloat16)
        prior_re = jnp.dot(prior_cols.T.astype(jnp.float32), wave_re.astype(jnp.float32), preferred_element_type=jnp.float32)
        prior_im = jnp.dot(prior_cols.T.astype(jnp.float32), wave_im.astype(jnp.float32), preferred_element_type=jnp.float32)
        window_phases = 2.0 * math.pi / NPHASE * window_seeds[freq_index].astype(jnp.float32)
        re_parts.append(prior_re + jnp.dot(factor, jnp.cos(window_phases), precision=lax.Precision.HIGHEST))
        im_parts.append(prior_im + jnp.dot(factor, jnp.sin(window_phases), precision=lax.Precision.HIGHEST))
    amp_re = jnp.stack(re_parts)
    amp_im = jnp.stack(im_parts)
    freq_bins = FIRST_BIN + jnp.arange(FREQS, dtype=jnp.int32)
    sample_ids = jnp.arange(STEPS, dtype=jnp.int32)
    turns = (freq_bins[:, None] * sample_ids[None, :] % STEPS).astype(jnp.float32) * (2.0 * math.pi / STEPS)
    first_sum = jnp.einsum('fps,ft->spt', amp_re, jnp.cos(turns), precision=lax.Precision.HIGHEST)
    second_sum = jnp.einsum('fps,ft->spt', amp_im, jnp.sin(turns), precision=lax.Precision.HIGHEST)
    natural = first_sum - second_sum
    stored = window_index(natural_ids, WINDOW, N_ROW * N_COL)
    return jnp.take(natural, stored, axis=1)
```

```python
import math

import jax
import jax.numpy as jnp
import numpy as np
from jax import lax
from jax.experimental import pallas as pl
from jax.experimental.pallas import tpu as pltpu
from jax.sharding import Mesh, PartitionSpec as P

GRID = 96
NPHASE = 4096
STEPS = 256
PRIOR = 26624
FIRST_BIN = 64
WINDOW = 1024
HALF = 512
SEEDS = 512
FREQS = 8
BLK = 128
CHIPS = 16
VMEM_BYTES = 40 * 1024 * 1024
EXACT = lax.Precision.HIGHEST

cross_weight = 0.3

FIRST = [(i, j) for j in range(4) for i in range(j + 1)]
SECOND = [(i, j) for j in range(4, 8) for i in range(j + 1)]
FIRST_ROWS = len(FIRST) * BLK // (2 * CHIPS)
SECOND_ROWS = len(SECOND) * BLK // (2 * CHIPS)
CHUNK = FIRST_ROWS + SECOND_ROWS

SINE = [(-1.0) ** i / math.factorial(2 * i + 1) for i in range(7)]


def params():
    return pltpu.CompilerParams(vmem_limit_bytes=VMEM_BYTES)


def pieces(local_block, rows):
    found = []
    at = 0
    while at < BLK:
        flat = local_block * BLK + at
        chip, inside = flat // rows, flat % rows
        length = min(rows - inside, BLK - at)
        found.append((at, chip, inside, length))
        at += length
    return found


def placed(blocks):
    half = len(blocks) // 2
    return [(pair, index // half, index % half) for index, pair in enumerate(blocks)]


def cosine(index):
    folded = jnp.abs(index - NPHASE // 2) - NPHASE // 4
    x = folded.astype(jnp.float32) * jnp.float32(2.0 * math.pi / NPHASE)
    y = x * x
    poly = jnp.full_like(x, SINE[-1])
    for c in SINE[-2::-1]:
        poly = poly * y + jnp.float32(c)
    return poly * x


def quarter_back(index):
    return (index + 3 * NPHASE // 4) & (NPHASE - 1)


def dot_t(a, b, precision=None):
    return lax.dot_general(a, b, (((0,), (0,)), ((), ())), preferred_element_type=jnp.float32, precision=precision)


def dot(a, b, precision=None):
    return jnp.dot(a, b, preferred_element_type=jnp.float32, precision=precision)


def schur_kernel(where_ref, cols_ref, keep_ref, send_ref):
    core = where_ref[0]
    spot = {}
    for offset, rows, blocks in ((0, FIRST_ROWS, FIRST), (FIRST_ROWS, SECOND_ROWS, SECOND)):
        for pair, half, local in placed(blocks):
            spot[pair] = (half, [(a, c, offset + i, n) for a, c, i, n in pieces(local, rows)])
    for i in range(8):
        product = dot_t(cols_ref[:, BLK * i : BLK * (i + 1)], cols_ref[:, BLK * i :])
        for j in range(i, 8):
            half, runs = spot[(i, j)]
            block = product[:, BLK * (j - i) : BLK * (j - i + 1)]

            @pl.when(core == half)
            def _():
                for at, chip, row, length in runs:
                    keep_ref[chip, row : row + length, :] = block[at : at + length, :]

            @pl.when(core != half)
            def _():
                for at, chip, row, length in runs:
                    send_ref[chip, row : row + length, :] = block[at : at + length, :]


def prior_kernel(cols_ref, seeds_ref, out_ref, waves_ref):
    for piece in range(SEEDS // BLK):
        lanes = slice(BLK * piece, BLK * (piece + 1))
        index = seeds_ref[:, lanes]
        waves_ref[:, lanes] = cosine(index).astype(jnp.bfloat16)
        waves_ref[:, SEEDS + BLK * piece : SEEDS + BLK * (piece + 1)] = cosine(quarter_back(index)).astype(jnp.bfloat16)
    for i in range(8):
        product = dot_t(cols_ref[:, BLK * i : BLK * (i + 1)], waves_ref[...])
        for part in range(8):
            owner = (8 * i + part) % 32
            row = 32 * owner + 16 * (i // 4)
            out_ref[row : row + 16, :] = product[16 * part : 16 * (part + 1), :]


def window_waves_kernel(seeds_ref, high_ref, low_ref):
    for piece in range(8):
        rows = slice(64 * piece, 64 * (piece + 1))
        lower = slice(SEEDS + 64 * piece, SEEDS + 64 * (piece + 1))
        index = seeds_ref[rows, :]
        for place, value in ((rows, cosine(index)), (lower, cosine(quarter_back(index)))):
            high = value.astype(jnp.bfloat16)
            high_ref[place, :] = high
            low_ref[place, :] = (value - high.astype(jnp.float32)).astype(jnp.bfloat16)


def bl(x, lane):
    return jnp.broadcast_to(x[:, lane : lane + 1], (8, BLK))


def bs(x, row):
    return jnp.broadcast_to(x[row : row + 1, :], (8, BLK))


def inverse_factor(rows):
    lane = lax.broadcasted_iota(jnp.int32, (8, BLK), 1)
    sub = lax.broadcasted_iota(jnp.int32, (8, BLK), 0)
    rows = list(rows)
    out = []
    for p in range(16):
        base = 8 * p
        inside = (lane >= base) & (lane < base + 8)
        here = rows[p]
        cols = [bl(here, base + k) for k in range(8)]
        a = [[bs(cols[k], i) if k >= i else None for k in range(8)] for i in range(8)]
        scale = []
        for j in range(8):
            s = lax.rsqrt(a[j][j])
            scale.append(s)
            for k in range(j + 1, 8):
                a[j][k] = a[j][k] * s
            for i in range(j + 1, 8):
                for k in range(i, 8):
                    a[i][k] = a[i][k] - a[j][i] * a[j][k]

        def forward(r):
            r = list(r)
            for j in range(8):
                r[j] = r[j] * scale[j]
                for i in range(j + 1, 8):
                    r[i] = r[i] - a[j][i] * r[j]
            return r

        eye = jnp.where(lane - base == sub, 1.0, 0.0)
        mixed = jnp.where(inside, eye, here)
        u = forward([bs(mixed, i) for i in range(8)])
        done = u[0]
        for j in range(1, 8):
            done = jnp.where(sub == j, u[j], done)
        out.append(jnp.where(lane < base + 8, done, 0.0))
        if p == 15:
            break
        n = forward([bl(rows[p + 1], base + j) for j in range(8)])
        t = [n[j] * u[j] for j in range(8)]
        t = (((t[0] + t[1]) + (t[2] + t[3])) + ((t[4] + t[5]) + t[6])) + t[7]
        rows[p + 1] = jnp.where(inside, 0.0, rows[p + 1]) - t
        if p == 14:
            continue
        w = [None] * 8
        for j in range(7, -1, -1):
            v = u[j]
            for k in range(j + 1, 8):
                v = v - a[j][k] * w[k]
            w[j] = v * scale[j]
        for r in range(p + 2, 16):
            v = jnp.where(inside, 0.0, rows[r])
            for j in range(8):
                v = v - bl(rows[r], base + j) * w[j]
            rows[r] = v
    return out


def factor_half(work_ref, upper_ref, inverse_ref, inverse_at):
    above = lax.broadcasted_iota(jnp.int32, (BLK, BLK), 0) <= lax.broadcasted_iota(jnp.int32, (BLK, BLK), 1)
    for k in range(4):
        top = BLK * k
        found = inverse_factor([work_ref[top + 8 * r : top + 8 * (r + 1), top : top + BLK] for r in range(16)])
        for r in range(16):
            inverse_ref[inverse_at + k, 8 * r : 8 * (r + 1), :] = found[r]
        row = dot(inverse_ref[inverse_at + k], work_ref[top : top + BLK, top:], EXACT)
        if k:
            upper_ref[top : top + BLK, :top] = jnp.zeros((BLK, top), jnp.float32)
        upper_ref[top : top + BLK, top : top + BLK] = jnp.where(above, row[:, :BLK], 0.0)
        if k < 3:
            upper_ref[top : top + BLK, top + BLK :] = row[:, BLK:]
        for i in range(k + 1, 4):
            work_ref[BLK * i : BLK * (i + 1), BLK * i :] -= dot_t(
                row[:, BLK * (i - k) : BLK * (i - k + 1)], row[:, BLK * (i - k) :], EXACT
            )


def unpack(core, own_ref, other_ref, blocks, rows, store):
    for pair, half, local in placed(blocks):
        for at, chip, inside, length in pieces(local, rows):
            span = slice(inside, inside + length)
            store(pair, at, length, jnp.where(core == half, own_ref[chip, span, :], other_ref[chip, span, :]))


def leading_kernel(where_ref, own_ref, other_ref, upper_ref, inverse_ref, work_ref):
    def store(pair, at, length, value):
        i, j = pair
        work_ref[BLK * i + at : BLK * i + at + length, BLK * j : BLK * (j + 1)] = value

    unpack(where_ref[0], own_ref, other_ref, FIRST, FIRST_ROWS, store)
    factor_half(work_ref, upper_ref, inverse_ref, 0)


def trailing_kernel(
    where_ref, own_ref, other_ref, upper_ref, inverse_ref, cross_ref, trailing_ref, side_ref, work_ref, spare_ref
):
    def store(pair, at, length, value):
        i, j = pair
        target, row = (side_ref, BLK * i) if i < 4 else (work_ref, BLK * (i - 4))
        target[row + at : row + at + length, BLK * (j - 4) : BLK * (j - 3)] = value

    unpack(where_ref[0], own_ref, other_ref, SECOND, SECOND_ROWS, store)
    for k in range(4):
        rows = slice(BLK * k, BLK * (k + 1))
        solved = dot(inverse_ref[k], side_ref[rows, :], EXACT)
        cross_ref[rows, :] = solved
        if k < 3:
            side_ref[BLK * (k + 1) :, :] -= dot_t(upper_ref[rows, BLK * (k + 1) :], solved, EXACT)
    for i in range(4):
        work_ref[BLK * i : BLK * (i + 1), BLK * i :] -= dot_t(
            cross_ref[:, BLK * i : BLK * (i + 1)], cross_ref[:, BLK * i :], EXACT
        )
    factor_half(work_ref, trailing_ref, spare_ref, 0)


def split(x):
    high = x.astype(jnp.bfloat16)
    return high, (x - high.astype(jnp.float32)).astype(jnp.bfloat16)


def amplitude_kernel(where_ref, upper_ref, cross_ref, trailing_ref, high_ref, low_ref, prior_ref, out_ref):
    owner = where_ref[1]
    start = pl.multiple_of(owner // 8 * BLK, BLK)
    shift = owner % 8 * 16
    column = lax.broadcasted_iota(jnp.int32, (BLK, BLK), 0)
    wanted = lax.broadcasted_iota(jnp.int32, (BLK, BLK), 1) % 32
    pick_first = jnp.where((wanted < 16) & (column == shift + wanted), 1.0, 0.0).astype(jnp.bfloat16)
    pick_second = jnp.where((wanted >= 16) & (column == shift + wanted - 16), 1.0, 0.0).astype(jnp.bfloat16)
    place = pl.ds(start, BLK)
    upper, cross, trailing = (split(r[:, place]) for r in (upper_ref, cross_ref, trailing_ref))
    mine = [
        jnp.concatenate(
            [
                (dot(upper[part], pick_first) + dot(cross[part], pick_second)).astype(jnp.bfloat16),
                dot(trailing[part], pick_second).astype(jnp.bfloat16),
            ],
            axis=0,
        )
        for part in range(2)
    ]
    repeat = jnp.where(
        lax.broadcasted_iota(jnp.int32, (32, BLK), 1) % 32 == lax.broadcasted_iota(jnp.int32, (32, BLK), 0), 1.0, 0.0
    )
    both = jnp.concatenate(mine, axis=1)
    group = lax.broadcasted_iota(jnp.int32, (16, BLK), 1) // 32
    for piece in range(8):
        rows = slice(BLK * piece, BLK * (piece + 1))
        wide = dot(high_ref[rows, :], both)
        amp = wide[:, :BLK] + wide[:, BLK:] + dot(low_ref[rows, :], mine[0])
        amp = amp + dot_t(prior_ref[:, rows], repeat, EXACT)
        for part in range(2):
            freq = 2 * (piece % 4) + part
            run = amp[64 * part : 64 * (part + 1), :]
            merged = run[:16]
            for s in range(1, 4):
                merged = jnp.where(group == s, run[16 * s : 16 * (s + 1)], merged)
            row = 16 * (piece // 4)
            out_ref[freq, row : row + 16, :] = merged


def synthesis_kernel(amp_ref, table_ref, out_ref):
    for s in range(16):
        lines = jnp.concatenate([amp_ref[:, s, :], amp_ref[:, 16 + s, :]], axis=0)
        series = dot_t(lines, table_ref[...], EXACT)
        for part in range(4):
            out_ref[16 * part + s] = series[32 * part : 32 * (part + 1), :]


SMEM = pl.BlockSpec(memory_space=pltpu.SMEM)
VMEM = pl.BlockSpec(memory_space=pltpu.VMEM)


def call(kernel, name, outs, ins, scratch=(), flops=0, moved=0):
    return pl.pallas_call(
        kernel,
        out_shape=outs,
        in_specs=ins,
        out_specs=jax.tree.map(lambda _: VMEM, outs),
        scratch_shapes=list(scratch),
        compiler_params=params(),
        cost_estimate=pl.CostEstimate(flops=flops, bytes_accessed=moved, transcendentals=0),
        name=name,
    )


def f32(*shape):
    return jax.ShapeDtypeStruct(shape, jnp.float32)


def lookup(table, index):
    result = jnp.zeros_like(index)
    for at, value in enumerate(table):
        result = jnp.where(index == at, value, result)
    return result


def coherence_chunk(spectra, nugget, decay, core, chip):
    rows, block_cols = [], []
    for count, blocks in ((FIRST_ROWS, FIRST), (SECOND_ROWS, SECOND)):
        flat = (core * CHIPS + chip) * count + jnp.arange(count, dtype=jnp.int32)
        block = flat // BLK
        rows.append(lookup([i for i, _ in blocks], block) * BLK + flat % BLK)
        block_cols.append(lookup([j for _, j in blocks], block))
    row_ids = jnp.concatenate(rows)
    block_col = jnp.concatenate(block_cols)
    col_ids = block_col[:, None] * BLK + jnp.arange(BLK, dtype=jnp.int32)[None, :]
    chosen = row_ids[:, None] == jnp.arange(WINDOW, dtype=jnp.int32)[None, :]
    row_spectra = jnp.sum(jnp.where(chosen, spectra[None, :], 0.0), axis=1)
    row_nugget = jnp.sum(jnp.where(chosen, nugget[None, :], 0.0), axis=1)
    by_block = spectra.reshape(8, BLK)
    col_spectra = jnp.zeros((CHUNK, BLK), jnp.float32)
    for j in range(8):
        col_spectra = jnp.where((block_col == j)[:, None], by_block[j][None, :], col_spectra)
    row_global = (PRIOR + row_ids)[:, None]
    col_global = PRIOR + col_ids
    row_points = row_global // 3
    col_points = col_global // 3
    across = (row_points % GRID - col_points % GRID).astype(jnp.float32)
    height = (row_points // GRID - col_points // GRID).astype(jnp.float32)
    distance = jnp.sqrt(across * across + height * height)
    coupling = jnp.where(row_global % 3 == col_global % 3, jnp.float32(1.0), jnp.float32(cross_weight))
    amplitude = jnp.sqrt(row_spectra[:, None] * col_spectra)
    diagonal = jnp.where(row_ids[:, None] == col_ids, row_nugget[:, None], jnp.float32(0.0))
    return coupling * amplitude * jnp.exp(-decay * distance) + diagonal


def tables():
    bins = FIRST_BIN + np.arange(FREQS)
    turns = (bins[:, None] * np.arange(STEPS)[None, :] % STEPS) * (2.0 * math.pi / STEPS)
    return jnp.asarray(np.concatenate([np.cos(turns), -np.sin(turns)], axis=0), jnp.float32)


CHIP_AXES = ("row", "y")


def exchange(x):
    return lax.all_to_all(x, CHIP_AXES, split_axis=0, concat_axis=0, tiled=True)


def swap(x):
    return lax.ppermute(x, "core", [(0, 1), (1, 0)])


def shards(prior_factor, prior_seeds, window_seeds, spectra, nugget, decay):
    cols = prior_factor[0]
    depth = cols.shape[0]
    core = lax.axis_index("core")
    chip = lax.axis_index(CHIP_AXES)
    owner = lax.axis_index(("row", "y", "core"))
    where = jnp.stack([core, owner]).astype(jnp.int32)

    with jax.named_scope("schur"):
        keep, send = call(
            schur_kernel, "schur", (f32(CHIPS, CHUNK, BLK),) * 2, [SMEM, VMEM], flops=10**9, moved=4 * 2**20
        )(where, cols)
        received = swap(send)
    with jax.named_scope("prior"):
        yields = call(
            prior_kernel,
            "prior",
            f32(WINDOW, 2 * SEEDS),
            [VMEM, VMEM],
            [pltpu.VMEM((depth, 2 * SEEDS), jnp.bfloat16)],
            flops=2 * 10**9,
            moved=8 * 2**20,
        )(cols, prior_seeds[0])
        prior = lax.psum_scatter(yields, ("row", "y", "core"), scatter_dimension=0, tiled=True)
    with jax.named_scope("reduce"):
        parts = exchange(keep + received)
        high, low = call(
            window_waves_kernel,
            "window_waves",
            (jax.ShapeDtypeStruct((2 * SEEDS, WINDOW), jnp.bfloat16),) * 2,
            [VMEM],
            flops=10**9,
            moved=6 * 2**20,
        )(window_seeds[0].T)
        known = coherence_chunk(spectra[0], nugget[0], decay[0], core, chip)
        chunk = known - jnp.sum(parts, axis=0)
    with jax.named_scope("gather_first"):
        own = exchange(jnp.broadcast_to(chunk[None, :FIRST_ROWS], (CHIPS, FIRST_ROWS, BLK)))
        other = swap(own)
    with jax.named_scope("gather_second"):
        rest, other = lax.optimization_barrier(
            (jnp.broadcast_to(chunk[None, FIRST_ROWS:], (CHIPS, SECOND_ROWS, BLK)), other)
        )
        own_rest = exchange(rest)
    with jax.named_scope("leading"):
        upper, inverse = call(
            leading_kernel,
            "leading",
            (f32(HALF, HALF), f32(4, BLK, BLK)),
            [SMEM, VMEM, VMEM],
            [pltpu.VMEM((HALF, HALF), jnp.float32)],
            flops=20 * 10**9,
            moved=2 * 2**20,
        )(where, own, other)
    with jax.named_scope("trailing"):
        other_rest = swap(own_rest)
        cross, trailing = call(
            trailing_kernel,
            "trailing",
            (f32(HALF, HALF), f32(HALF, HALF)),
            [SMEM, VMEM, VMEM, VMEM, VMEM],
            [pltpu.VMEM((HALF, HALF), jnp.float32)] * 2 + [pltpu.VMEM((4, BLK, BLK), jnp.float32)],
            flops=25 * 10**9,
            moved=4 * 2**20,
        )(where, own_rest, other_rest, upper, inverse)
    with jax.named_scope("amplitude"):
        amp = call(
            amplitude_kernel,
            "amplitude",
            f32(FREQS, 32, BLK),
            [SMEM] + [VMEM] * 6,
            flops=10**9,
            moved=8 * 2**20,
        )(where, upper, cross, trailing, high, low, prior)
        amp = lax.all_to_all(amp, "freq", split_axis=0, concat_axis=0, tiled=True)
    with jax.named_scope("synthesis"):
        return call(synthesis_kernel, "synthesis", f32(64, 32, STEPS), [VMEM, VMEM], flops=10**8, moved=2 * 2**20)(
            amp, tables()
        )


def solution(mesh):
    chips = Mesh(mesh.devices.reshape(8, 4, 4, 2), ("freq", "row", "y", "core"))
    own = ("row", "y", "core")
    in_specs = (
        P("freq", own, None),
        P("freq", own, None),
        P("freq", None, None),
        P("freq", None),
        P("freq", None),
        P("freq"),
    )
    return jax.shard_map(shards, mesh=chips, in_specs=in_specs, out_specs=P("freq", own, None), check_vma=False)
```

```python
import math

import jax
import jax.numpy as jnp
import numpy as np
from jax import lax
from jax.experimental import pallas as pl
from jax.experimental.pallas import tpu as pltpu
from jax.sharding import Mesh, PartitionSpec as P

GRID = 96
NPHASE = 4096
STEPS = 256
PRIOR = 26624
FIRST_BIN = 64
WINDOW = 1024
HALF = 512
SEEDS = 512
FREQS = 8
BLK = 128
CHIPS = 16
VMEM_BYTES = 16 * 1024 * 1024
VMEM_LAST = 20 * 1024 * 1024
EXACT = lax.Precision.HIGHEST

cross_weight = 0.3

FIRST = [(i, j) for j in range(4) for i in range(j + 1)]
SECOND = [(i, j) for j in range(4, 8) for i in range(j + 1)]
FIRST_ROWS = len(FIRST) * BLK // (2 * CHIPS)
SECOND_ROWS = len(SECOND) * BLK // (2 * CHIPS)
CHUNK = FIRST_ROWS + SECOND_ROWS

SINE = [(-1.0) ** i / math.factorial(2 * i + 1) for i in range(7)]


def pieces(local_block, rows):
    found = []
    at = 0
    while at < BLK:
        flat = local_block * BLK + at
        chip, inside = flat // rows, flat % rows
        length = min(rows - inside, BLK - at)
        found.append((at, chip, inside, length))
        at += length
    return found


def placed(blocks):
    half = len(blocks) // 2
    return [(pair, index // half, index % half) for index, pair in enumerate(blocks)]


def cosine(index):
    folded = jnp.abs(index - NPHASE // 2) - NPHASE // 4
    x = folded.astype(jnp.float32) * jnp.float32(2.0 * math.pi / NPHASE)
    y = x * x
    poly = jnp.full_like(x, SINE[-1])
    for c in SINE[-2::-1]:
        poly = poly * y + jnp.float32(c)
    return poly * x


def quarter_back(index):
    return (index + 3 * NPHASE // 4) & (NPHASE - 1)


def dot_t(a, b, precision=None):
    return lax.dot_general(a, b, (((0,), (0,)), ((), ())), preferred_element_type=jnp.float32, precision=precision)


def dot(a, b, precision=None):
    return jnp.dot(a, b, preferred_element_type=jnp.float32, precision=precision)


def schur_kernel(where_ref, cols_ref, keep_ref, send_ref):
    core = where_ref[0]
    spot = {}
    for offset, rows, blocks in ((0, FIRST_ROWS, FIRST), (FIRST_ROWS, SECOND_ROWS, SECOND)):
        for pair, half, local in placed(blocks):
            spot[pair] = (half, [(a, c, offset + i, n) for a, c, i, n in pieces(local, rows)])
    for i in range(8):
        product = dot_t(cols_ref[:, BLK * i : BLK * (i + 1)], cols_ref[:, BLK * i :])
        for j in range(i, 8):
            half, runs = spot[(i, j)]
            block = product[:, BLK * (j - i) : BLK * (j - i + 1)]

            @pl.when(core == half)
            def _():
                for at, chip, row, length in runs:
                    keep_ref[chip, row : row + length, :] = block[at : at + length, :]

            @pl.when(core != half)
            def _():
                for at, chip, row, length in runs:
                    send_ref[chip, row : row + length, :] = block[at : at + length, :]


def prior_kernel(where_ref, cols_ref, seeds_ref, keep_ref, send_ref, waves_ref):
    core = where_ref[0]
    for piece in range(SEEDS // BLK):
        lanes = slice(BLK * piece, BLK * (piece + 1))
        index = seeds_ref[:, lanes]
        waves_ref[:, lanes] = cosine(index).astype(jnp.bfloat16)
        waves_ref[:, SEEDS + BLK * piece : SEEDS + BLK * (piece + 1)] = cosine(quarter_back(index)).astype(jnp.bfloat16)
    for i in range(8):
        product = dot_t(cols_ref[:, BLK * i : BLK * (i + 1)], waves_ref[...])

        def store(half, target):
            for part in range(half, 8, 2):
                row = 32 * ((8 * i + part) % 32 // 2) + 16 * (i // 4)
                target[row : row + 16, :] = product[16 * part : 16 * (part + 1), :]

        @pl.when(core == 0)
        def _():
            store(0, keep_ref)
            store(1, send_ref)

        @pl.when(core != 0)
        def _():
            store(1, keep_ref)
            store(0, send_ref)


def window_waves_kernel(seeds_ref, high_ref, low_ref):
    for piece in range(8):
        rows = slice(64 * piece, 64 * (piece + 1))
        lower = slice(SEEDS + 64 * piece, SEEDS + 64 * (piece + 1))
        index = seeds_ref[rows, :]
        for place, value in ((rows, cosine(index)), (lower, cosine(quarter_back(index)))):
            high = value.astype(jnp.bfloat16)
            high_ref[place, :] = high
            low_ref[place, :] = (value - high.astype(jnp.float32)).astype(jnp.bfloat16)


def bl(x, lane):
    return jnp.broadcast_to(x[:, lane : lane + 1], (8, BLK))


def bs(x, row):
    return jnp.broadcast_to(x[row : row + 1, :], (8, BLK))


def inverse_factor(rows):
    lane = lax.broadcasted_iota(jnp.int32, (8, BLK), 1)
    sub = lax.broadcasted_iota(jnp.int32, (8, BLK), 0)
    rows = list(rows)
    out = []
    for p in range(16):
        base = 8 * p
        inside = (lane >= base) & (lane < base + 8)
        here = rows[p]
        cols = [bl(here, base + k) for k in range(8)]
        a = [[bs(cols[k], i) if k >= i else None for k in range(8)] for i in range(8)]
        scale = []
        for j in range(8):
            s = lax.rsqrt(a[j][j])
            scale.append(s)
            for k in range(j + 1, 8):
                a[j][k] = a[j][k] * s
            for i in range(j + 1, 8):
                for k in range(i, 8):
                    a[i][k] = a[i][k] - a[j][i] * a[j][k]

        def forward(r):
            r = list(r)
            for j in range(8):
                r[j] = r[j] * scale[j]
                for i in range(j + 1, 8):
                    r[i] = r[i] - a[j][i] * r[j]
            return r

        eye = jnp.where(lane - base == sub, 1.0, 0.0)
        mixed = jnp.where(inside, eye, here)
        u = forward([bs(mixed, i) for i in range(8)])
        done = u[0]
        for j in range(1, 8):
            done = jnp.where(sub == j, u[j], done)
        out.append(jnp.where(lane < base + 8, done, 0.0))
        if p == 15:
            break
        n = forward([bl(rows[p + 1], base + j) for j in range(8)])
        t = [n[j] * u[j] for j in range(8)]
        t = (((t[0] + t[1]) + (t[2] + t[3])) + ((t[4] + t[5]) + t[6])) + t[7]
        rows[p + 1] = jnp.where(inside, 0.0, rows[p + 1]) - t
        if p == 14:
            continue
        w = [None] * 8
        for j in range(7, -1, -1):
            v = u[j]
            for k in range(j + 1, 8):
                v = v - a[j][k] * w[k]
            w[j] = v * scale[j]
        for r in range(p + 2, 16):
            v = jnp.where(inside, 0.0, rows[r])
            for j in range(8):
                v = v - bl(rows[r], base + j) * w[j]
            rows[r] = v
    return out


def factor_blocks(work_ref, upper_ref, inverse_ref, first, last, count):
    above = lax.broadcasted_iota(jnp.int32, (BLK, BLK), 0) <= lax.broadcasted_iota(jnp.int32, (BLK, BLK), 1)
    for k in range(first, last):
        top = BLK * k
        found = inverse_factor([work_ref[top + 8 * r : top + 8 * (r + 1), top : top + BLK] for r in range(16)])
        for r in range(16):
            inverse_ref[k - first, 8 * r : 8 * (r + 1), :] = found[r]
        row = dot(inverse_ref[k - first], work_ref[top : top + BLK, top:], EXACT)
        if k:
            upper_ref[top : top + BLK, :top] = jnp.zeros((BLK, top), jnp.float32)
        upper_ref[top : top + BLK, top : top + BLK] = jnp.where(above, row[:, :BLK], 0.0)
        if k < count - 1:
            upper_ref[top : top + BLK, top + BLK :] = row[:, BLK:]
        for i in range(k + 1, count):
            work_ref[BLK * i : BLK * (i + 1), BLK * i :] -= dot_t(
                row[:, BLK * (i - k) : BLK * (i - k + 1)], row[:, BLK * (i - k) :], EXACT
            )


def unpack(core, own_ref, other_ref, blocks, rows, store):
    for pair, half, local in placed(blocks):
        for at, chip, inside, length in pieces(local, rows):
            span = slice(inside, inside + length)
            store(pair, at, length, jnp.where(core == half, own_ref[chip, span, :], other_ref[chip, span, :]))


def leading_kernel(where_ref, own_ref, other_ref, upper_ref, inverse_ref, left_ref, work_ref):
    def store(pair, at, length, value):
        i, j = pair
        work_ref[BLK * i + at : BLK * i + at + length, BLK * j : BLK * (j + 1)] = value

    unpack(where_ref[0], own_ref, other_ref, FIRST, FIRST_ROWS, store)
    factor_blocks(work_ref, upper_ref, inverse_ref, 0, 3, 4)
    left_ref[...] = work_ref[3 * BLK :, 3 * BLK :]


def corner_kernel(left_ref, upper_ref, inverse_ref):
    factor_blocks(left_ref, upper_ref, inverse_ref, 0, 1, 1)


def cross_kernel(
    where_ref, own_ref, other_ref, upper_ref, inverse_ref, corner_inverse_ref, cross_ref, work_ref, side_ref
):
    def store(pair, at, length, value):
        i, j = pair
        target, row = (side_ref, BLK * i) if i < 4 else (work_ref, BLK * (i - 4))
        target[row + at : row + at + length, BLK * (j - 4) : BLK * (j - 3)] = value

    unpack(where_ref[0], own_ref, other_ref, SECOND, SECOND_ROWS, store)
    for k in range(4):
        rows = slice(BLK * k, BLK * (k + 1))
        inverse = inverse_ref[k] if k < 3 else corner_inverse_ref[0]
        solved = dot(inverse, side_ref[rows, :], EXACT)
        cross_ref[rows, :] = solved
        if k < 3:
            side_ref[BLK * (k + 1) :, :] -= dot_t(upper_ref[rows, BLK * (k + 1) :], solved, EXACT)
    for i in range(4):
        if i:
            work_ref[BLK * i : BLK * (i + 1), : BLK * i] = jnp.zeros((BLK, BLK * i), jnp.float32)
        work_ref[BLK * i : BLK * (i + 1), BLK * i :] -= dot_t(
            cross_ref[:, BLK * i : BLK * (i + 1)], cross_ref[:, BLK * i :], EXACT
        )


def trailing_kernel(
    where_ref,
    start_ref,
    upper_ref,
    corner_ref,
    cross_ref,
    high_ref,
    low_ref,
    prior_ref,
    out_ref,
    work_ref,
    trailing_ref,
    spare_ref,
    full_ref,
    high_here,
    low_here,
    prior_here,
    semaphores,
):
    fetches = [
        pltpu.make_async_copy(source, target, semaphores.at[i])
        for i, (source, target) in enumerate(((high_ref, high_here), (low_ref, low_here), (prior_ref, prior_here)))
    ]
    for fetch in fetches:
        fetch.start()
    work_ref[...] = start_ref[...]
    factor_blocks(work_ref, trailing_ref, spare_ref, 0, 4, 4)
    last = slice(3 * BLK, 4 * BLK)
    full_ref[: 3 * BLK, :] = upper_ref[...]
    full_ref[last, : 3 * BLK] = jnp.zeros((BLK, 3 * BLK), jnp.float32)
    full_ref[last, last] = corner_ref[...]
    for fetch in fetches:
        fetch.wait()
    amplitude(where_ref[1], full_ref, cross_ref, trailing_ref, high_here, low_here, prior_here, out_ref)


def split(x):
    high = x.astype(jnp.bfloat16)
    return high, (x - high.astype(jnp.float32)).astype(jnp.bfloat16)


def amplitude(owner, upper_ref, cross_ref, trailing_ref, high_ref, low_ref, prior_ref, out_ref):
    start = pl.multiple_of(owner // 8 * BLK, BLK)
    shift = owner % 8 * 16
    column = lax.broadcasted_iota(jnp.int32, (BLK, BLK), 0)
    wanted = lax.broadcasted_iota(jnp.int32, (BLK, BLK), 1) % 32
    pick_first = jnp.where((wanted < 16) & (column == shift + wanted), 1.0, 0.0).astype(jnp.bfloat16)
    pick_second = jnp.where((wanted >= 16) & (column == shift + wanted - 16), 1.0, 0.0).astype(jnp.bfloat16)
    place = pl.ds(start, BLK)
    upper, cross, trailing = (split(r[:, place]) for r in (upper_ref, cross_ref, trailing_ref))
    mine = [
        jnp.concatenate(
            [
                (dot(upper[part], pick_first) + dot(cross[part], pick_second)).astype(jnp.bfloat16),
                dot(trailing[part], pick_second).astype(jnp.bfloat16),
            ],
            axis=0,
        )
        for part in range(2)
    ]
    repeat = jnp.where(
        lax.broadcasted_iota(jnp.int32, (32, BLK), 1) % 32 == lax.broadcasted_iota(jnp.int32, (32, BLK), 0), 1.0, 0.0
    )
    both = jnp.concatenate(mine, axis=1)
    group = lax.broadcasted_iota(jnp.int32, (16, BLK), 1) // 32
    for piece in range(8):
        rows = slice(BLK * piece, BLK * (piece + 1))
        wide = dot(high_ref[rows, :], both)
        amp = wide[:, :BLK] + wide[:, BLK:] + dot(low_ref[rows, :], mine[0])
        amp = amp + dot_t(prior_ref[:, rows], repeat, EXACT)
        for part in range(2):
            freq = 2 * (piece % 4) + part
            run = amp[64 * part : 64 * (part + 1), :]
            merged = run[:16]
            for s in range(1, 4):
                merged = jnp.where(group == s, run[16 * s : 16 * (s + 1)], merged)
            row = 16 * (piece // 4)
            out_ref[freq, row : row + 16, :] = merged


def synthesis_kernel(amp_ref, table_ref, out_ref):
    for s in range(16):
        lines = jnp.concatenate([amp_ref[:, s, :], amp_ref[:, 16 + s, :]], axis=0)
        series = dot_t(lines, table_ref[...], EXACT)
        for part in range(4):
            out_ref[16 * part + s] = series[32 * part : 32 * (part + 1), :]


SMEM = pl.BlockSpec(memory_space=pltpu.SMEM)
VMEM = pl.BlockSpec(memory_space=pltpu.VMEM)
HBM = pl.BlockSpec(memory_space=pltpu.HBM)


def call(kernel, name, outs, ins, scratch=(), flops=0, moved=0, vmem=VMEM_BYTES):
    return pl.pallas_call(
        kernel,
        out_shape=outs,
        in_specs=ins,
        out_specs=jax.tree.map(lambda _: VMEM, outs),
        scratch_shapes=list(scratch),
        compiler_params=pltpu.CompilerParams(vmem_limit_bytes=vmem),
        cost_estimate=pl.CostEstimate(flops=flops, bytes_accessed=moved, transcendentals=0),
        name=name,
    )


def f32(*shape):
    return jax.ShapeDtypeStruct(shape, jnp.float32)


def lookup(table, index):
    result = jnp.zeros_like(index)
    for at, value in enumerate(table):
        result = jnp.where(index == at, value, result)
    return result


def coherence_chunk(spectra, nugget, decay, core, chip):
    rows, block_cols = [], []
    for count, blocks in ((FIRST_ROWS, FIRST), (SECOND_ROWS, SECOND)):
        flat = (core * CHIPS + chip) * count + jnp.arange(count, dtype=jnp.int32)
        block = flat // BLK
        rows.append(lookup([i for i, _ in blocks], block) * BLK + flat % BLK)
        block_cols.append(lookup([j for _, j in blocks], block))
    row_ids = jnp.concatenate(rows)
    block_col = jnp.concatenate(block_cols)
    col_ids = block_col[:, None] * BLK + jnp.arange(BLK, dtype=jnp.int32)[None, :]
    chosen = row_ids[:, None] == jnp.arange(WINDOW, dtype=jnp.int32)[None, :]
    row_spectra = jnp.sum(jnp.where(chosen, spectra[None, :], 0.0), axis=1)
    row_nugget = jnp.sum(jnp.where(chosen, nugget[None, :], 0.0), axis=1)
    by_block = spectra.reshape(8, BLK)
    col_spectra = jnp.zeros((CHUNK, BLK), jnp.float32)
    for j in range(8):
        col_spectra = jnp.where((block_col == j)[:, None], by_block[j][None, :], col_spectra)
    row_global = (PRIOR + row_ids)[:, None]
    col_global = PRIOR + col_ids
    row_points = row_global // 3
    col_points = col_global // 3
    across = (row_points % GRID - col_points % GRID).astype(jnp.float32)
    height = (row_points // GRID - col_points // GRID).astype(jnp.float32)
    distance = jnp.sqrt(across * across + height * height)
    coupling = jnp.where(row_global % 3 == col_global % 3, jnp.float32(1.0), jnp.float32(cross_weight))
    amplitude = jnp.sqrt(row_spectra[:, None] * col_spectra)
    diagonal = jnp.where(row_ids[:, None] == col_ids, row_nugget[:, None], jnp.float32(0.0))
    return coupling * amplitude * jnp.exp(-decay * distance) + diagonal


def tables():
    bins = FIRST_BIN + np.arange(FREQS)
    turns = (bins[:, None] * np.arange(STEPS)[None, :] % STEPS) * (2.0 * math.pi / STEPS)
    return jnp.asarray(np.concatenate([np.cos(turns), -np.sin(turns)], axis=0), jnp.float32)


CHIP_AXES = ("row", "y")


def exchange(x):
    return lax.all_to_all(x, CHIP_AXES, split_axis=0, concat_axis=0, tiled=True)


def swap(x):
    return lax.ppermute(x, "core", [(0, 1), (1, 0)])


def scatter_ring(x):
    place = lax.axis_index("y")
    blocks = x.reshape(4, x.shape[0] // 4, x.shape[1])
    total = lax.dynamic_index_in_dim(blocks, place, 0, keepdims=False)
    for step in range(1, 4):
        away = lax.dynamic_index_in_dim(blocks, (place + step) % 4, 0, keepdims=False)
        total = total + lax.ppermute(away, "y", [(i, (i + step) % 4) for i in range(4)])
    return total


def shards(prior_factor, prior_seeds, window_seeds, spectra, nugget, decay):
    cols = prior_factor[0]
    depth = cols.shape[0]
    core = lax.axis_index("core")
    chip = lax.axis_index(CHIP_AXES)
    owner = lax.axis_index(("row", "y", "core"))
    where = jnp.stack([core, owner]).astype(jnp.int32)

    with jax.named_scope("prior"):
        yield_keep, yield_send = call(
            prior_kernel,
            "prior",
            (f32(WINDOW // 2, 2 * SEEDS),) * 2,
            [SMEM, VMEM, VMEM],
            [pltpu.VMEM((depth, 2 * SEEDS), jnp.bfloat16)],
            flops=2 * 10**9,
            moved=8 * 2**20,
        )(where, cols, prior_seeds[0])
        yield_send, cols = lax.optimization_barrier((yield_send, cols))
        prior = lax.psum_scatter(yield_keep + swap(yield_send), "row", scatter_dimension=0, tiled=True)
    with jax.named_scope("schur"):
        keep, send = call(
            schur_kernel, "schur", (f32(CHIPS, CHUNK, BLK),) * 2, [SMEM, VMEM], flops=10**9, moved=4 * 2**20
        )(where, cols)
        received = swap(send)
    with jax.named_scope("reduce"):
        summed, window_index = lax.optimization_barrier((keep + received, window_seeds[0]))
        parts = exchange(summed)
        high, low = call(
            window_waves_kernel,
            "window_waves",
            (jax.ShapeDtypeStruct((2 * SEEDS, WINDOW), jnp.bfloat16),) * 2,
            [VMEM],
            flops=1000,
            moved=1000,
        )(window_index.T)
        known = coherence_chunk(spectra[0], nugget[0], decay[0], core, chip)
        chunk = known - jnp.sum(parts, axis=0)
        chunk, high, low = lax.optimization_barrier((chunk, high, low))
    with jax.named_scope("gather_first"):
        own = exchange(jnp.broadcast_to(chunk[None, :FIRST_ROWS], (CHIPS, FIRST_ROWS, BLK)))
        other = swap(own)
    with jax.named_scope("gather_second"):
        rest, other = lax.optimization_barrier(
            (jnp.broadcast_to(chunk[None, FIRST_ROWS:], (CHIPS, SECOND_ROWS, BLK)), other)
        )
        own_rest = exchange(rest)
    with jax.named_scope("leading"):
        upper, inverse, left = call(
            leading_kernel,
            "leading",
            (f32(HALF - BLK, HALF), f32(3, BLK, BLK), f32(BLK, BLK)),
            [SMEM, VMEM, VMEM],
            [pltpu.VMEM((HALF, HALF), jnp.float32)],
            flops=20 * 10**9,
            moved=2 * 2**20,
        )(where, own, other)
    with jax.named_scope("gather_last"):
        own_rest, prior, left = lax.optimization_barrier((own_rest, prior, left))
        other_rest = swap(own_rest)
        prior = scatter_ring(prior)
    with jax.named_scope("corner"):
        corner, corner_inverse = call(
            corner_kernel, "corner", (f32(BLK, BLK), f32(1, BLK, BLK)), [VMEM], flops=6 * 10**9, moved=2**17
        )(left)
    square = pltpu.VMEM((HALF, HALF), jnp.float32)
    with jax.named_scope("cross"):
        cross, work = call(
            cross_kernel,
            "cross",
            (f32(HALF, HALF),) * 2,
            [SMEM] + [VMEM] * 5,
            [square],
            flops=7 * 10**9,
            moved=4 * 2**20,
        )(where, own_rest, other_rest, upper, inverse, corner_inverse)
    with jax.named_scope("trailing"):
        prior, work = lax.optimization_barrier((prior, work))
        amp = call(
            trailing_kernel,
            "trailing",
            f32(FREQS, 32, BLK),
            [SMEM] + [VMEM] * 4 + [HBM] * 3,
            [square] * 2
            + [pltpu.VMEM((4, BLK, BLK), jnp.float32), square]
            + [pltpu.VMEM((2 * SEEDS, WINDOW), jnp.bfloat16)] * 2
            + [pltpu.VMEM((32, 2 * SEEDS), jnp.float32), pltpu.SemaphoreType.DMA((3,))],
            flops=25 * 10**9,
            moved=4 * 2**20,
            vmem=VMEM_LAST,
        )(where, work, upper, corner, cross, high, low, prior)
    with jax.named_scope("amplitude"):
        amp = lax.all_to_all(amp, "freq", split_axis=0, concat_axis=0, tiled=True)
    with jax.named_scope("synthesis"):
        return call(synthesis_kernel, "synthesis", f32(64, 32, STEPS), [VMEM, VMEM], flops=10**8, moved=2 * 2**20)(
            amp, tables()
        )


def solution(mesh):
    chips = Mesh(mesh.devices.reshape(8, 4, 4, 2), ("freq", "row", "y", "core"))
    own = ("row", "y", "core")
    in_specs = (
        P("freq", own, None),
        P("freq", own, None),
        P("freq", None, None),
        P("freq", None),
        P("freq", None),
        P("freq"),
    )
    return jax.shard_map(shards, mesh=chips, in_specs=in_specs, out_specs=P("freq", own, None), check_vma=False)
```

```python
import math

import jax
import jax.numpy as jnp
import numpy as np
from jax import lax
from jax.experimental import pallas as pl
from jax.experimental.pallas import tpu as pltpu
from jax.sharding import Mesh, PartitionSpec as P

GRID = 96
NPHASE = 4096
STEPS = 256
PRIOR = 26624
FIRST_BIN = 64
WINDOW = 1024
HALF = 512
SEEDS = 512
FREQS = 8
BLK = 128
CHIPS = 16
VMEM_BYTES = 16 * 1024 * 1024
VMEM_LAST = 20 * 1024 * 1024
EXACT = lax.Precision.HIGHEST

cross_weight = 0.3

FIRST = [(i, j) for j in range(4) for i in range(j + 1)]
SECOND = [(i, j) for j in range(4, 8) for i in range(j + 1)]
FIRST_ROWS = len(FIRST) * BLK // (2 * CHIPS)
SECOND_ROWS = len(SECOND) * BLK // (2 * CHIPS)
CHUNK = FIRST_ROWS + SECOND_ROWS

SINE = [(-1.0) ** i / math.factorial(2 * i + 1) for i in range(7)]


def pieces(local_block, rows):
    found = []
    at = 0
    while at < BLK:
        flat = local_block * BLK + at
        chip, inside = flat // rows, flat % rows
        length = min(rows - inside, BLK - at)
        found.append((at, chip, inside, length))
        at += length
    return found


def placed(blocks):
    half = len(blocks) // 2
    return [(pair, index // half, index % half) for index, pair in enumerate(blocks)]


def cosine(index):
    folded = jnp.abs(index - NPHASE // 2) - NPHASE // 4
    x = folded.astype(jnp.float32) * jnp.float32(2.0 * math.pi / NPHASE)
    y = x * x
    poly = jnp.full_like(x, SINE[-1])
    for c in SINE[-2::-1]:
        poly = poly * y + jnp.float32(c)
    return poly * x


def quarter_back(index):
    return (index + 3 * NPHASE // 4) & (NPHASE - 1)


def dot_t(a, b, precision=None):
    return lax.dot_general(a, b, (((0,), (0,)), ((), ())), preferred_element_type=jnp.float32, precision=precision)


def dot(a, b, precision=None):
    return jnp.dot(a, b, preferred_element_type=jnp.float32, precision=precision)


def schur_kernel(where_ref, cols_ref, keep_ref, send_ref):
    core = where_ref[0]
    spot = {}
    for offset, rows, blocks in ((0, FIRST_ROWS, FIRST), (FIRST_ROWS, SECOND_ROWS, SECOND)):
        for pair, half, local in placed(blocks):
            spot[pair] = (half, [(a, c, offset + i, n) for a, c, i, n in pieces(local, rows)])
    for i in range(8):
        product = dot_t(cols_ref[:, BLK * i : BLK * (i + 1)], cols_ref[:, BLK * i :])
        for j in range(i, 8):
            half, runs = spot[(i, j)]
            block = product[:, BLK * (j - i) : BLK * (j - i + 1)]

            @pl.when(core == half)
            def _():
                for at, chip, row, length in runs:
                    keep_ref[chip, row : row + length, :] = block[at : at + length, :]

            @pl.when(core != half)
            def _():
                for at, chip, row, length in runs:
                    send_ref[chip, row : row + length, :] = block[at : at + length, :]


def prior_kernel(where_ref, cols_ref, seeds_ref, keep_ref, send_ref, waves_ref):
    core = where_ref[0]
    for piece in range(SEEDS // BLK):
        lanes = slice(BLK * piece, BLK * (piece + 1))
        index = seeds_ref[:, lanes]
        waves_ref[:, lanes] = cosine(index).astype(jnp.bfloat16)
        waves_ref[:, SEEDS + BLK * piece : SEEDS + BLK * (piece + 1)] = cosine(quarter_back(index)).astype(jnp.bfloat16)
    for i in range(8):
        product = dot_t(cols_ref[:, BLK * i : BLK * (i + 1)], waves_ref[...])

        def store(half, target):
            for part in range(half, 8, 2):
                row = 32 * ((8 * i + part) % 32 // 2) + 16 * (i // 4)
                target[row : row + 16, :] = product[16 * part : 16 * (part + 1), :]

        @pl.when(core == 0)
        def _():
            store(0, keep_ref)
            store(1, send_ref)

        @pl.when(core != 0)
        def _():
            store(1, keep_ref)
            store(0, send_ref)


def window_waves_kernel(seeds_ref, high_ref, low_ref):
    for piece in range(8):
        rows = slice(64 * piece, 64 * (piece + 1))
        lower = slice(SEEDS + 64 * piece, SEEDS + 64 * (piece + 1))
        index = seeds_ref[rows, :]
        for place, value in ((rows, cosine(index)), (lower, cosine(quarter_back(index)))):
            high = value.astype(jnp.bfloat16)
            high_ref[place, :] = high
            low_ref[place, :] = (value - high.astype(jnp.float32)).astype(jnp.bfloat16)


def bl(x, lane):
    return jnp.broadcast_to(x[:, lane : lane + 1], (8, BLK))


def bs(x, row):
    return jnp.broadcast_to(x[row : row + 1, :], (8, BLK))


def inverse_factor(rows):
    lane = lax.broadcasted_iota(jnp.int32, (8, BLK), 1)
    sub = lax.broadcasted_iota(jnp.int32, (8, BLK), 0)
    rows = list(rows)
    out = []
    for p in range(16):
        base = 8 * p
        inside = (lane >= base) & (lane < base + 8)
        here = rows[p]
        cols = [bl(here, base + k) for k in range(8)]
        a = [[bs(cols[k], i) if k >= i else None for k in range(8)] for i in range(8)]
        scale = []
        for j in range(8):
            s = lax.rsqrt(a[j][j])
            scale.append(s)
            for k in range(j + 1, 8):
                a[j][k] = a[j][k] * s
            for i in range(j + 1, 8):
                for k in range(i, 8):
                    a[i][k] = a[i][k] - a[j][i] * a[j][k]

        def forward(r):
            r = list(r)
            for j in range(8):
                r[j] = r[j] * scale[j]
                for i in range(j + 1, 8):
                    r[i] = r[i] - a[j][i] * r[j]
            return r

        eye = jnp.where(lane - base == sub, 1.0, 0.0)
        mixed = jnp.where(inside, eye, here)
        u = forward([bs(mixed, i) for i in range(8)])
        done = u[0]
        for j in range(1, 8):
            done = jnp.where(sub == j, u[j], done)
        out.append(jnp.where(lane < base + 8, done, 0.0))
        if p == 15:
            break
        n = forward([bl(rows[p + 1], base + j) for j in range(8)])
        t = [n[j] * u[j] for j in range(8)]
        t = (((t[0] + t[1]) + (t[2] + t[3])) + ((t[4] + t[5]) + t[6])) + t[7]
        rows[p + 1] = jnp.where(inside, 0.0, rows[p + 1]) - t
        if p == 14:
            continue
        w = [None] * 8
        for j in range(7, -1, -1):
            v = u[j]
            for k in range(j + 1, 8):
                v = v - a[j][k] * w[k]
            w[j] = v * scale[j]
        for r in range(p + 2, 16):
            v = jnp.where(inside, 0.0, rows[r])
            for j in range(8):
                v = v - bl(rows[r], base + j) * w[j]
            rows[r] = v
    return out


def factor_blocks(work_ref, upper_ref, inverse_ref, first, last, count):
    above = lax.broadcasted_iota(jnp.int32, (BLK, BLK), 0) <= lax.broadcasted_iota(jnp.int32, (BLK, BLK), 1)
    for k in range(first, last):
        top = BLK * k
        found = inverse_factor([work_ref[top + 8 * r : top + 8 * (r + 1), top : top + BLK] for r in range(16)])
        for r in range(16):
            inverse_ref[k - first, 8 * r : 8 * (r + 1), :] = found[r]
        row = dot(inverse_ref[k - first], work_ref[top : top + BLK, top:], EXACT)
        if k:
            upper_ref[top : top + BLK, :top] = jnp.zeros((BLK, top), jnp.float32)
        upper_ref[top : top + BLK, top : top + BLK] = jnp.where(above, row[:, :BLK], 0.0)
        if k < count - 1:
            upper_ref[top : top + BLK, top + BLK :] = row[:, BLK:]
        for i in range(k + 1, count):
            work_ref[BLK * i : BLK * (i + 1), BLK * i :] -= dot_t(
                row[:, BLK * (i - k) : BLK * (i - k + 1)], row[:, BLK * (i - k) :], EXACT
            )


def unpack(core, own_ref, other_ref, blocks, rows, store):
    for pair, half, local in placed(blocks):
        for at, chip, inside, length in pieces(local, rows):
            span = slice(inside, inside + length)
            store(pair, at, length, jnp.where(core == half, own_ref[chip, span, :], other_ref[chip, span, :]))


def leading_kernel(where_ref, own_ref, other_ref, upper_ref, inverse_ref, left_ref, work_ref):
    def store(pair, at, length, value):
        i, j = pair
        work_ref[BLK * i + at : BLK * i + at + length, BLK * j : BLK * (j + 1)] = value

    unpack(where_ref[0], own_ref, other_ref, FIRST, FIRST_ROWS, store)
    factor_blocks(work_ref, upper_ref, inverse_ref, 0, 3, 4)
    left_ref[...] = work_ref[3 * BLK :, 3 * BLK :]


def corner_kernel(left_ref, upper_ref, inverse_ref):
    factor_blocks(left_ref, upper_ref, inverse_ref, 0, 1, 1)


def cross_kernel(
    where_ref, own_ref, other_ref, upper_ref, inverse_ref, corner_inverse_ref, cross_ref, work_ref, side_ref
):
    def store(pair, at, length, value):
        i, j = pair
        target, row = (side_ref, BLK * i) if i < 4 else (work_ref, BLK * (i - 4))
        target[row + at : row + at + length, BLK * (j - 4) : BLK * (j - 3)] = value

    unpack(where_ref[0], own_ref, other_ref, SECOND, SECOND_ROWS, store)
    for k in range(4):
        rows = slice(BLK * k, BLK * (k + 1))
        inverse = inverse_ref[k] if k < 3 else corner_inverse_ref[0]
        solved = dot(inverse, side_ref[rows, :], EXACT)
        cross_ref[rows, :] = solved
        if k < 3:
            side_ref[BLK * (k + 1) :, :] -= dot_t(upper_ref[rows, BLK * (k + 1) :], solved, EXACT)
    for i in range(4):
        if i:
            work_ref[BLK * i : BLK * (i + 1), : BLK * i] = jnp.zeros((BLK, BLK * i), jnp.float32)
        work_ref[BLK * i : BLK * (i + 1), BLK * i :] -= dot_t(
            cross_ref[:, BLK * i : BLK * (i + 1)], cross_ref[:, BLK * i :], EXACT
        )


def trailing_kernel(
    where_ref,
    start_ref,
    upper_ref,
    corner_ref,
    cross_ref,
    high_ref,
    low_ref,
    out_ref,
    work_ref,
    trailing_ref,
    spare_ref,
    full_ref,
    high_here,
    low_here,
    semaphores,
):
    fetches = [
        pltpu.make_async_copy(source, target, semaphores.at[i])
        for i, (source, target) in enumerate(((high_ref, high_here), (low_ref, low_here)))
    ]
    for fetch in fetches:
        fetch.start()
    work_ref[...] = start_ref[...]
    factor_blocks(work_ref, trailing_ref, spare_ref, 0, 4, 4)
    last = slice(3 * BLK, 4 * BLK)
    full_ref[: 3 * BLK, :] = upper_ref[...]
    full_ref[last, : 3 * BLK] = jnp.zeros((BLK, 3 * BLK), jnp.float32)
    full_ref[last, last] = corner_ref[...]
    for fetch in fetches:
        fetch.wait()
    amplitude(where_ref[1], full_ref, cross_ref, trailing_ref, high_here, low_here, out_ref)


def split(x):
    high = x.astype(jnp.bfloat16)
    return high, (x - high.astype(jnp.float32)).astype(jnp.bfloat16)


def amplitude(owner, upper_ref, cross_ref, trailing_ref, high_ref, low_ref, out_ref):
    start = pl.multiple_of(owner // 8 * BLK, BLK)
    shift = owner % 8 * 16
    column = lax.broadcasted_iota(jnp.int32, (BLK, BLK), 0)
    wanted = lax.broadcasted_iota(jnp.int32, (BLK, BLK), 1) % 32
    pick_first = jnp.where((wanted < 16) & (column == shift + wanted), 1.0, 0.0).astype(jnp.bfloat16)
    pick_second = jnp.where((wanted >= 16) & (column == shift + wanted - 16), 1.0, 0.0).astype(jnp.bfloat16)
    place = pl.ds(start, BLK)
    upper, cross, trailing = (split(r[:, place]) for r in (upper_ref, cross_ref, trailing_ref))
    mine = [
        jnp.concatenate(
            [
                (dot(upper[part], pick_first) + dot(cross[part], pick_second)).astype(jnp.bfloat16),
                dot(trailing[part], pick_second).astype(jnp.bfloat16),
            ],
            axis=0,
        )
        for part in range(2)
    ]
    both = jnp.concatenate(mine, axis=1)
    for piece in range(8):
        rows = slice(BLK * piece, BLK * (piece + 1))
        wide = dot(high_ref[rows, :], both)
        fold(piece, wide[:, :BLK] + wide[:, BLK:] + dot(low_ref[rows, :], mine[0]), out_ref)


def fold(piece, amp, out_ref):
    group = lax.broadcasted_iota(jnp.int32, (16, BLK), 1) // 32
    for part in range(2):
        run = amp[64 * part : 64 * (part + 1), :]
        merged = run[:16]
        for s in range(1, 4):
            merged = jnp.where(group == s, run[16 * s : 16 * (s + 1)], merged)
        row = 16 * (piece // 4)
        out_ref[2 * (piece % 4) + part, row : row + 16, :] = merged


def finish_kernel(amp_ref, parts_ref, out_ref, total_ref):
    repeat = jnp.where(
        lax.broadcasted_iota(jnp.int32, (32, BLK), 1) % 32 == lax.broadcasted_iota(jnp.int32, (32, BLK), 0), 1.0, 0.0
    )
    for piece in range(8):
        lanes = slice(BLK * piece, BLK * (piece + 1))
        fold(piece, dot_t(jnp.sum(parts_ref[:, :, lanes], axis=0), repeat, EXACT), total_ref)
    out_ref[...] = amp_ref[...] + total_ref[...]


def synthesis_kernel(amp_ref, table_ref, out_ref):
    for s in range(16):
        lines = jnp.concatenate([amp_ref[:, s, :], amp_ref[:, 16 + s, :]], axis=0)
        series = dot_t(lines, table_ref[...], EXACT)
        for part in range(4):
            out_ref[16 * part + s] = series[32 * part : 32 * (part + 1), :]


SMEM = pl.BlockSpec(memory_space=pltpu.SMEM)
VMEM = pl.BlockSpec(memory_space=pltpu.VMEM)
HBM = pl.BlockSpec(memory_space=pltpu.HBM)


def call(kernel, name, outs, ins, scratch=(), flops=0, moved=0, vmem=VMEM_BYTES):
    return pl.pallas_call(
        kernel,
        out_shape=outs,
        in_specs=ins,
        out_specs=jax.tree.map(lambda _: VMEM, outs),
        scratch_shapes=list(scratch),
        compiler_params=pltpu.CompilerParams(vmem_limit_bytes=vmem),
        cost_estimate=pl.CostEstimate(flops=flops, bytes_accessed=moved, transcendentals=0),
        name=name,
    )


def f32(*shape):
    return jax.ShapeDtypeStruct(shape, jnp.float32)


def lookup(table, index):
    result = jnp.zeros_like(index)
    for at, value in enumerate(table):
        result = jnp.where(index == at, value, result)
    return result


def coherence_chunk(spectra, nugget, decay, core, chip):
    rows, block_cols = [], []
    for count, blocks in ((FIRST_ROWS, FIRST), (SECOND_ROWS, SECOND)):
        flat = (core * CHIPS + chip) * count + jnp.arange(count, dtype=jnp.int32)
        block = flat // BLK
        rows.append(lookup([i for i, _ in blocks], block) * BLK + flat % BLK)
        block_cols.append(lookup([j for _, j in blocks], block))
    row_ids = jnp.concatenate(rows)
    block_col = jnp.concatenate(block_cols)
    col_ids = block_col[:, None] * BLK + jnp.arange(BLK, dtype=jnp.int32)[None, :]
    chosen = row_ids[:, None] == jnp.arange(WINDOW, dtype=jnp.int32)[None, :]
    row_spectra = jnp.sum(jnp.where(chosen, spectra[None, :], 0.0), axis=1)
    row_nugget = jnp.sum(jnp.where(chosen, nugget[None, :], 0.0), axis=1)
    by_block = spectra.reshape(8, BLK)
    col_spectra = jnp.zeros((CHUNK, BLK), jnp.float32)
    for j in range(8):
        col_spectra = jnp.where((block_col == j)[:, None], by_block[j][None, :], col_spectra)
    row_global = (PRIOR + row_ids)[:, None]
    col_global = PRIOR + col_ids
    row_points = row_global // 3
    col_points = col_global // 3
    across = (row_points % GRID - col_points % GRID).astype(jnp.float32)
    height = (row_points // GRID - col_points // GRID).astype(jnp.float32)
    distance = jnp.sqrt(across * across + height * height)
    coupling = jnp.where(row_global % 3 == col_global % 3, jnp.float32(1.0), jnp.float32(cross_weight))
    amplitude = jnp.sqrt(row_spectra[:, None] * col_spectra)
    diagonal = jnp.where(row_ids[:, None] == col_ids, row_nugget[:, None], jnp.float32(0.0))
    return coupling * amplitude * jnp.exp(-decay * distance) + diagonal


def tables():
    bins = FIRST_BIN + np.arange(FREQS)
    turns = (bins[:, None] * np.arange(STEPS)[None, :] % STEPS) * (2.0 * math.pi / STEPS)
    return jnp.asarray(np.concatenate([np.cos(turns), -np.sin(turns)], axis=0), jnp.float32)


CHIP_AXES = ("row", "y")


def exchange(x):
    return lax.all_to_all(x, CHIP_AXES, split_axis=0, concat_axis=0, tiled=True)


def swap(x):
    return lax.ppermute(x, "core", [(0, 1), (1, 0)])


def shards(prior_factor, prior_seeds, window_seeds, spectra, nugget, decay):
    cols = prior_factor[0]
    depth = cols.shape[0]
    core = lax.axis_index("core")
    chip = lax.axis_index(CHIP_AXES)
    owner = lax.axis_index(("row", "y", "core"))
    where = jnp.stack([core, owner]).astype(jnp.int32)

    with jax.named_scope("schur"):
        keep, send = call(
            schur_kernel, "schur", (f32(CHIPS, CHUNK, BLK),) * 2, [SMEM, VMEM], flops=10**9, moved=4 * 2**20
        )(where, cols)
        send, seeds = lax.optimization_barrier((send, prior_seeds[0]))
        received = swap(send)
    with jax.named_scope("prior"):
        yield_keep, yield_send = call(
            prior_kernel,
            "prior",
            (f32(WINDOW // 2, 2 * SEEDS),) * 2,
            [SMEM, VMEM, VMEM],
            [pltpu.VMEM((depth, 2 * SEEDS), jnp.bfloat16)],
            flops=2 * 10**9,
            moved=8 * 2**20,
        )(where, cols, seeds)
    with jax.named_scope("reduce"):
        summed, window_index, yield_keep, yield_send = lax.optimization_barrier(
            (keep + received, window_seeds[0], yield_keep, yield_send)
        )
        parts = exchange(summed)
        yield_received = swap(yield_send)
    with jax.named_scope("window"):
        high, low = call(
            window_waves_kernel,
            "window_waves",
            (jax.ShapeDtypeStruct((2 * SEEDS, WINDOW), jnp.bfloat16),) * 2,
            [VMEM],
            flops=1000,
            moved=1000,
        )(window_index.T)
    with jax.named_scope("known"):
        known = coherence_chunk(spectra[0], nugget[0], decay[0], core, chip)
        known, high, low = lax.optimization_barrier((known, high, low))
        chunk = known - jnp.sum(parts, axis=0)
        chunk, yield_keep, yield_received = lax.optimization_barrier((chunk, yield_keep, yield_received))
        prior = yield_keep + yield_received
    with jax.named_scope("gather_first"):
        own = exchange(jnp.broadcast_to(chunk[None, :FIRST_ROWS], (CHIPS, FIRST_ROWS, BLK)))
        own, prior = lax.optimization_barrier((own, prior))
        other = swap(own)
    with jax.named_scope("gather_second"):
        rest, other = lax.optimization_barrier(
            (jnp.broadcast_to(chunk[None, FIRST_ROWS:], (CHIPS, SECOND_ROWS, BLK)), other)
        )
        own_rest = exchange(rest)
    with jax.named_scope("leading"):
        upper, inverse, left = call(
            leading_kernel,
            "leading",
            (f32(HALF - BLK, HALF), f32(3, BLK, BLK), f32(BLK, BLK)),
            [SMEM, VMEM, VMEM],
            [pltpu.VMEM((HALF, HALF), jnp.float32)],
            flops=20 * 10**9,
            moved=2 * 2**20,
        )(where, own, other)
    with jax.named_scope("gather_last"):
        own_rest, prior, left = lax.optimization_barrier((own_rest, prior, left))
        other_rest = swap(own_rest)
        prior_parts = exchange(prior.reshape(CHIPS, 32, 2 * SEEDS))
    with jax.named_scope("corner"):
        corner, corner_inverse = call(
            corner_kernel, "corner", (f32(BLK, BLK), f32(1, BLK, BLK)), [VMEM], flops=6 * 10**9, moved=2**17
        )(left)
    square = pltpu.VMEM((HALF, HALF), jnp.float32)
    with jax.named_scope("cross"):
        cross, work = call(
            cross_kernel,
            "cross",
            (f32(HALF, HALF),) * 2,
            [SMEM] + [VMEM] * 5,
            [square],
            flops=7 * 10**9,
            moved=4 * 2**20,
        )(where, own_rest, other_rest, upper, inverse, corner_inverse)
    with jax.named_scope("trailing"):
        amp = call(
            trailing_kernel,
            "trailing",
            f32(FREQS, 32, BLK),
            [SMEM] + [VMEM] * 4 + [HBM] * 2,
            [square] * 2
            + [pltpu.VMEM((4, BLK, BLK), jnp.float32), square]
            + [pltpu.VMEM((2 * SEEDS, WINDOW), jnp.bfloat16)] * 2
            + [pltpu.SemaphoreType.DMA((2,))],
            flops=25 * 10**9,
            moved=4 * 2**20,
            vmem=VMEM_LAST,
        )(where, work, upper, corner, cross, high, low)
    with jax.named_scope("amplitude"):
        amp = call(
            finish_kernel,
            "finish",
            f32(FREQS, 32, BLK),
            [VMEM, VMEM],
            [pltpu.VMEM((FREQS, 32, BLK), jnp.float32)],
            flops=10**8,
            moved=2 * 2**20,
        )(amp, prior_parts)
        amp = lax.all_to_all(amp, "freq", split_axis=0, concat_axis=0, tiled=True)
    with jax.named_scope("synthesis"):
        return call(synthesis_kernel, "synthesis", f32(64, 32, STEPS), [VMEM, VMEM], flops=10**8, moved=2 * 2**20)(
            amp, tables()
        )


def solution(mesh):
    chips = Mesh(mesh.devices.reshape(8, 4, 4, 2), ("freq", "row", "y", "core"))
    own = ("row", "y", "core")
    in_specs = (
        P("freq", own, None),
        P("freq", own, None),
        P("freq", None, None),
        P("freq", None),
        P("freq", None),
        P("freq"),
    )
    return jax.shard_map(shards, mesh=chips, in_specs=in_specs, out_specs=P("freq", own, None), check_vma=False)
```

```python
import math

import jax
import jax.numpy as jnp
import numpy as np
from jax import lax
from jax.experimental import pallas as pl
from jax.experimental.pallas import tpu as pltpu
from jax.sharding import Mesh, PartitionSpec as P

GRID = 96
NPHASE = 4096
STEPS = 256
PRIOR = 26624
FIRST_BIN = 64
WINDOW = 1024
HALF = 512
SEEDS = 512
FREQS = 8
BLK = 128
CHIPS = 16
VMEM_BYTES = 16 * 1024 * 1024
VMEM_LAST = 20 * 1024 * 1024
EXACT = lax.Precision.HIGHEST

cross_weight = 0.3

FIRST = [(i, j) for j in range(4) for i in range(j + 1)]
SECOND = [(i, j) for j in range(4, 8) for i in range(j + 1)]
FIRST_ROWS = len(FIRST) * BLK // (2 * CHIPS)
SECOND_ROWS = len(SECOND) * BLK // (2 * CHIPS)
CHUNK = FIRST_ROWS + SECOND_ROWS

SINE = [(-1.0) ** i / math.factorial(2 * i + 1) for i in range(7)]


def pieces(local_block, rows):
    found = []
    at = 0
    while at < BLK:
        flat = local_block * BLK + at
        chip, inside = flat // rows, flat % rows
        length = min(rows - inside, BLK - at)
        found.append((at, chip, inside, length))
        at += length
    return found


def placed(blocks):
    half = len(blocks) // 2
    return [(pair, index // half, index % half) for index, pair in enumerate(blocks)]


def cosine(index):
    folded = jnp.abs(index - NPHASE // 2) - NPHASE // 4
    x = folded.astype(jnp.float32) * jnp.float32(2.0 * math.pi / NPHASE)
    y = x * x
    poly = jnp.full_like(x, SINE[-1])
    for c in SINE[-2::-1]:
        poly = poly * y + jnp.float32(c)
    return poly * x


def quarter_back(index):
    return (index + 3 * NPHASE // 4) & (NPHASE - 1)


def dot_t(a, b, precision=None):
    return lax.dot_general(a, b, (((0,), (0,)), ((), ())), preferred_element_type=jnp.float32, precision=precision)


def dot(a, b, precision=None):
    return jnp.dot(a, b, preferred_element_type=jnp.float32, precision=precision)


def schur_kernel(where_ref, cols_ref, keep_ref, send_ref):
    core = where_ref[0]
    spot = {}
    for offset, rows, blocks in ((0, FIRST_ROWS, FIRST), (FIRST_ROWS, SECOND_ROWS, SECOND)):
        for pair, half, local in placed(blocks):
            spot[pair] = (half, [(a, c, offset + i, n) for a, c, i, n in pieces(local, rows)])
    for i in range(8):
        product = dot_t(cols_ref[:, BLK * i : BLK * (i + 1)], cols_ref[:, BLK * i :])
        for j in range(i, 8):
            half, runs = spot[(i, j)]
            block = product[:, BLK * (j - i) : BLK * (j - i + 1)]

            @pl.when(core == half)
            def _():
                for at, chip, row, length in runs:
                    keep_ref[chip, row : row + length, :] = block[at : at + length, :]

            @pl.when(core != half)
            def _():
                for at, chip, row, length in runs:
                    send_ref[chip, row : row + length, :] = block[at : at + length, :]


def prior_kernel(where_ref, cols_ref, seeds_ref, keep_ref, send_ref, waves_ref):
    core = where_ref[0]
    for piece in range(SEEDS // BLK):
        lanes = slice(BLK * piece, BLK * (piece + 1))
        index = seeds_ref[:, lanes]
        waves_ref[:, lanes] = cosine(index).astype(jnp.bfloat16)
        waves_ref[:, SEEDS + BLK * piece : SEEDS + BLK * (piece + 1)] = cosine(quarter_back(index)).astype(jnp.bfloat16)
    for i in range(8):
        product = dot_t(cols_ref[:, BLK * i : BLK * (i + 1)], waves_ref[...])

        def store(half, target):
            for part in range(half, 8, 2):
                row = 32 * ((8 * i + part) % 32 // 2) + 16 * (i // 4)
                target[row : row + 16, :] = product[16 * part : 16 * (part + 1), :]

        @pl.when(core == 0)
        def _():
            store(0, keep_ref)
            store(1, send_ref)

        @pl.when(core != 0)
        def _():
            store(1, keep_ref)
            store(0, send_ref)


def window_waves_kernel(seeds_ref, high_ref, low_ref):
    for piece in range(8):
        rows = slice(64 * piece, 64 * (piece + 1))
        lower = slice(SEEDS + 64 * piece, SEEDS + 64 * (piece + 1))
        index = seeds_ref[rows, :]
        for place, value in ((rows, cosine(index)), (lower, cosine(quarter_back(index)))):
            high = value.astype(jnp.bfloat16)
            high_ref[place, :] = high
            low_ref[place, :] = (value - high.astype(jnp.float32)).astype(jnp.bfloat16)


def bl(x, lane):
    return jnp.broadcast_to(x[:, lane : lane + 1], (8, BLK))


def bs(x, row):
    return jnp.broadcast_to(x[row : row + 1, :], (8, BLK))


def inverse_factor(rows):
    lane = lax.broadcasted_iota(jnp.int32, (8, BLK), 1)
    sub = lax.broadcasted_iota(jnp.int32, (8, BLK), 0)
    rows = list(rows)
    out = []
    cols = [bl(rows[0], k) for k in range(8)]
    for p in range(16):
        base = 8 * p
        inside = (lane >= base) & (lane < base + 8)
        here = rows[p]
        a = [[bs(cols[k], i) if k >= i else None for k in range(8)] for i in range(8)]
        scale = []
        for j in range(8):
            s = lax.rsqrt(a[j][j])
            scale.append(s)
            for k in range(j + 1, 8):
                a[j][k] = a[j][k] * s
            for i in range(j + 1, 8):
                for k in range(i, 8):
                    a[i][k] = a[i][k] - a[j][i] * a[j][k]

        def forward(r):
            r = list(r)
            for j in range(8):
                r[j] = r[j] * scale[j]
                for i in range(j + 1, 8):
                    r[i] = r[i] - a[j][i] * r[j]
            return r

        eye = jnp.where(lane - base == sub, 1.0, 0.0)
        mixed = jnp.where(inside, eye, here)
        u = forward([bs(mixed, i) for i in range(8)])
        done = u[0]
        for j in range(1, 8):
            done = jnp.where(sub == j, u[j], done)
        out.append(jnp.where(lane < base + 8, done, 0.0))
        if p == 15:
            break
        n = forward([bl(rows[p + 1], base + j) for j in range(8)])
        cols = []
        for k in range(8):
            t = [n[j] * bs(n[j], k) for j in range(8)]
            t = ((t[0] + t[1]) + (t[2] + t[3])) + ((t[4] + t[5]) + t[6]) + t[7]
            cols.append(bl(rows[p + 1], base + 8 + k) - t)
        t = [n[j] * u[j] for j in range(8)]
        t = (((t[0] + t[1]) + (t[2] + t[3])) + ((t[4] + t[5]) + t[6])) + t[7]
        rows[p + 1] = jnp.where(inside, 0.0, rows[p + 1]) - t
        if p == 14:
            continue
        w = [None] * 8
        for j in range(7, -1, -1):
            v = u[j]
            for k in range(j + 1, 8):
                v = v - a[j][k] * w[k]
            w[j] = v * scale[j]
        for r in range(p + 2, 16):
            v = jnp.where(inside, 0.0, rows[r])
            for j in range(8):
                v = v - bl(rows[r], base + j) * w[j]
            rows[r] = v
    return out


def factor_blocks(work_ref, upper_ref, inverse_ref, first, last, count):
    above = lax.broadcasted_iota(jnp.int32, (BLK, BLK), 0) <= lax.broadcasted_iota(jnp.int32, (BLK, BLK), 1)
    for k in range(first, last):
        top = BLK * k
        found = inverse_factor([work_ref[top + 8 * r : top + 8 * (r + 1), top : top + BLK] for r in range(16)])
        for r in range(16):
            inverse_ref[k - first, 8 * r : 8 * (r + 1), :] = found[r]
        row = dot(inverse_ref[k - first], work_ref[top : top + BLK, top:], EXACT)
        if k:
            upper_ref[top : top + BLK, :top] = jnp.zeros((BLK, top), jnp.float32)
        upper_ref[top : top + BLK, top : top + BLK] = jnp.where(above, row[:, :BLK], 0.0)
        if k < count - 1:
            upper_ref[top : top + BLK, top + BLK :] = row[:, BLK:]
        for i in range(k + 1, count):
            work_ref[BLK * i : BLK * (i + 1), BLK * i :] -= dot_t(
                row[:, BLK * (i - k) : BLK * (i - k + 1)], row[:, BLK * (i - k) :], EXACT
            )


def unpack(core, own_ref, other_ref, blocks, rows, store):
    for pair, half, local in placed(blocks):
        for at, chip, inside, length in pieces(local, rows):
            span = slice(inside, inside + length)
            store(pair, at, length, jnp.where(core == half, own_ref[chip, span, :], other_ref[chip, span, :]))


def leading_kernel(where_ref, own_ref, other_ref, upper_ref, inverse_ref, left_ref, work_ref):
    def store(pair, at, length, value):
        i, j = pair
        work_ref[BLK * i + at : BLK * i + at + length, BLK * j : BLK * (j + 1)] = value

    unpack(where_ref[0], own_ref, other_ref, FIRST, FIRST_ROWS, store)
    factor_blocks(work_ref, upper_ref, inverse_ref, 0, 3, 4)
    left_ref[...] = work_ref[3 * BLK :, 3 * BLK :]


def corner_kernel(left_ref, upper_ref, inverse_ref):
    factor_blocks(left_ref, upper_ref, inverse_ref, 0, 1, 1)


def cross_kernel(
    where_ref, own_ref, other_ref, upper_ref, inverse_ref, corner_inverse_ref, cross_ref, work_ref, side_ref
):
    def store(pair, at, length, value):
        i, j = pair
        target, row = (side_ref, BLK * i) if i < 4 else (work_ref, BLK * (i - 4))
        target[row + at : row + at + length, BLK * (j - 4) : BLK * (j - 3)] = value

    unpack(where_ref[0], own_ref, other_ref, SECOND, SECOND_ROWS, store)
    for k in range(4):
        rows = slice(BLK * k, BLK * (k + 1))
        inverse = inverse_ref[k] if k < 3 else corner_inverse_ref[0]
        solved = dot(inverse, side_ref[rows, :], EXACT)
        cross_ref[rows, :] = solved
        if k < 3:
            side_ref[BLK * (k + 1) :, :] -= dot_t(upper_ref[rows, BLK * (k + 1) :], solved, EXACT)
    for i in range(4):
        if i:
            work_ref[BLK * i : BLK * (i + 1), : BLK * i] = jnp.zeros((BLK, BLK * i), jnp.float32)
        work_ref[BLK * i : BLK * (i + 1), BLK * i :] -= dot_t(
            cross_ref[:, BLK * i : BLK * (i + 1)], cross_ref[:, BLK * i :], EXACT
        )


def trailing_kernel(
    where_ref,
    start_ref,
    upper_ref,
    corner_ref,
    cross_ref,
    high_ref,
    low_ref,
    out_ref,
    work_ref,
    trailing_ref,
    spare_ref,
    full_ref,
    high_here,
    low_here,
    semaphores,
):
    fetches = [
        pltpu.make_async_copy(source, target, semaphores.at[i])
        for i, (source, target) in enumerate(((high_ref, high_here), (low_ref, low_here)))
    ]
    for fetch in fetches:
        fetch.start()
    work_ref[...] = start_ref[...]
    factor_blocks(work_ref, trailing_ref, spare_ref, 0, 4, 4)
    last = slice(3 * BLK, 4 * BLK)
    full_ref[: 3 * BLK, :] = upper_ref[...]
    full_ref[last, : 3 * BLK] = jnp.zeros((BLK, 3 * BLK), jnp.float32)
    full_ref[last, last] = corner_ref[...]
    for fetch in fetches:
        fetch.wait()
    amplitude(where_ref[1], full_ref, cross_ref, trailing_ref, high_here, low_here, out_ref)


def split(x):
    high = x.astype(jnp.bfloat16)
    return high, (x - high.astype(jnp.float32)).astype(jnp.bfloat16)


def amplitude(owner, upper_ref, cross_ref, trailing_ref, high_ref, low_ref, out_ref):
    start = pl.multiple_of(owner // 8 * BLK, BLK)
    shift = owner % 8 * 16
    column = lax.broadcasted_iota(jnp.int32, (BLK, BLK), 0)
    wanted = lax.broadcasted_iota(jnp.int32, (BLK, BLK), 1) % 32
    pick_first = jnp.where((wanted < 16) & (column == shift + wanted), 1.0, 0.0).astype(jnp.bfloat16)
    pick_second = jnp.where((wanted >= 16) & (column == shift + wanted - 16), 1.0, 0.0).astype(jnp.bfloat16)
    place = pl.ds(start, BLK)
    upper, cross, trailing = (split(r[:, place]) for r in (upper_ref, cross_ref, trailing_ref))
    mine = [
        jnp.concatenate(
            [
                (dot(upper[part], pick_first) + dot(cross[part], pick_second)).astype(jnp.bfloat16),
                dot(trailing[part], pick_second).astype(jnp.bfloat16),
            ],
            axis=0,
        )
        for part in range(2)
    ]
    both = jnp.concatenate(mine, axis=1)
    for piece in range(8):
        rows = slice(BLK * piece, BLK * (piece + 1))
        wide = dot(high_ref[rows, :], both)
        fold(piece, wide[:, :BLK] + wide[:, BLK:] + dot(low_ref[rows, :], mine[0]), out_ref)


def fold(piece, amp, out_ref):
    group = lax.broadcasted_iota(jnp.int32, (16, BLK), 1) // 32
    for part in range(2):
        run = amp[64 * part : 64 * (part + 1), :]
        merged = run[:16]
        for s in range(1, 4):
            merged = jnp.where(group == s, run[16 * s : 16 * (s + 1)], merged)
        row = 16 * (piece // 4)
        out_ref[2 * (piece % 4) + part, row : row + 16, :] = merged


def finish_kernel(amp_ref, parts_ref, out_ref, total_ref):
    repeat = jnp.where(
        lax.broadcasted_iota(jnp.int32, (32, BLK), 1) % 32 == lax.broadcasted_iota(jnp.int32, (32, BLK), 0), 1.0, 0.0
    )
    for piece in range(8):
        lanes = slice(BLK * piece, BLK * (piece + 1))
        fold(piece, dot_t(jnp.sum(parts_ref[:, :, lanes], axis=0), repeat, EXACT), total_ref)
    out_ref[...] = amp_ref[...] + total_ref[...]


def synthesis_kernel(amp_ref, table_ref, out_ref):
    for s in range(16):
        lines = jnp.concatenate([amp_ref[:, s, :], amp_ref[:, 16 + s, :]], axis=0)
        series = dot_t(lines, table_ref[...], EXACT)
        for part in range(4):
            out_ref[16 * part + s] = series[32 * part : 32 * (part + 1), :]


SMEM = pl.BlockSpec(memory_space=pltpu.SMEM)
VMEM = pl.BlockSpec(memory_space=pltpu.VMEM)
HBM = pl.BlockSpec(memory_space=pltpu.HBM)


def call(kernel, name, outs, ins, scratch=(), flops=0, moved=0, vmem=VMEM_BYTES):
    return pl.pallas_call(
        kernel,
        out_shape=outs,
        in_specs=ins,
        out_specs=jax.tree.map(lambda _: VMEM, outs),
        scratch_shapes=list(scratch),
        compiler_params=pltpu.CompilerParams(vmem_limit_bytes=vmem),
        cost_estimate=pl.CostEstimate(flops=flops, bytes_accessed=moved, transcendentals=0),
        name=name,
    )


def f32(*shape):
    return jax.ShapeDtypeStruct(shape, jnp.float32)


def lookup(table, index):
    result = jnp.zeros_like(index)
    for at, value in enumerate(table):
        result = jnp.where(index == at, value, result)
    return result


def coherence_chunk(spectra, nugget, decay, core, chip):
    rows, block_cols = [], []
    for count, blocks in ((FIRST_ROWS, FIRST), (SECOND_ROWS, SECOND)):
        flat = (core * CHIPS + chip) * count + jnp.arange(count, dtype=jnp.int32)
        block = flat // BLK
        rows.append(lookup([i for i, _ in blocks], block) * BLK + flat % BLK)
        block_cols.append(lookup([j for _, j in blocks], block))
    row_ids = jnp.concatenate(rows)
    block_col = jnp.concatenate(block_cols)
    col_ids = block_col[:, None] * BLK + jnp.arange(BLK, dtype=jnp.int32)[None, :]
    chosen = row_ids[:, None] == jnp.arange(WINDOW, dtype=jnp.int32)[None, :]
    row_spectra = jnp.sum(jnp.where(chosen, spectra[None, :], 0.0), axis=1)
    row_nugget = jnp.sum(jnp.where(chosen, nugget[None, :], 0.0), axis=1)
    by_block = spectra.reshape(8, BLK)
    col_spectra = jnp.zeros((CHUNK, BLK), jnp.float32)
    for j in range(8):
        col_spectra = jnp.where((block_col == j)[:, None], by_block[j][None, :], col_spectra)
    row_global = (PRIOR + row_ids)[:, None]
    col_global = PRIOR + col_ids
    row_points = row_global // 3
    col_points = col_global // 3
    across = (row_points % GRID - col_points % GRID).astype(jnp.float32)
    height = (row_points // GRID - col_points // GRID).astype(jnp.float32)
    distance = jnp.sqrt(across * across + height * height)
    coupling = jnp.where(row_global % 3 == col_global % 3, jnp.float32(1.0), jnp.float32(cross_weight))
    amplitude = jnp.sqrt(row_spectra[:, None] * col_spectra)
    diagonal = jnp.where(row_ids[:, None] == col_ids, row_nugget[:, None], jnp.float32(0.0))
    return coupling * amplitude * jnp.exp(-decay * distance) + diagonal


def tables():
    bins = FIRST_BIN + np.arange(FREQS)
    turns = (bins[:, None] * np.arange(STEPS)[None, :] % STEPS) * (2.0 * math.pi / STEPS)
    return jnp.asarray(np.concatenate([np.cos(turns), -np.sin(turns)], axis=0), jnp.float32)


CHIP_AXES = ("row", "y")


def exchange(x):
    return lax.all_to_all(x, CHIP_AXES, split_axis=0, concat_axis=0, tiled=True)


def swap(x):
    return lax.ppermute(x, "core", [(0, 1), (1, 0)])


def shards(prior_factor, prior_seeds, window_seeds, spectra, nugget, decay):
    cols = prior_factor[0]
    depth = cols.shape[0]
    core = lax.axis_index("core")
    chip = lax.axis_index(CHIP_AXES)
    owner = lax.axis_index(("row", "y", "core"))
    where = jnp.stack([core, owner]).astype(jnp.int32)

    with jax.named_scope("schur"):
        keep, send = call(
            schur_kernel, "schur", (f32(CHIPS, CHUNK, BLK),) * 2, [SMEM, VMEM], flops=10**9, moved=4 * 2**20
        )(where, cols)
        send, window_index = lax.optimization_barrier((send, window_seeds[0]))
        received = swap(send)
        turned = window_index.T
    with jax.named_scope("reduce"):
        summed, turned, seeds = lax.optimization_barrier((keep + received, turned, prior_seeds[0]))
        parts = exchange(summed)
    with jax.named_scope("prior"):
        yield_keep, yield_send = call(
            prior_kernel,
            "prior",
            (f32(WINDOW // 2, 2 * SEEDS),) * 2,
            [SMEM, VMEM, VMEM],
            [pltpu.VMEM((depth, 2 * SEEDS), jnp.bfloat16)],
            flops=1000,
            moved=1000,
        )(where, cols, seeds)
    with jax.named_scope("window"):
        high, low = call(
            window_waves_kernel,
            "window_waves",
            (jax.ShapeDtypeStruct((2 * SEEDS, WINDOW), jnp.bfloat16),) * 2,
            [VMEM],
            flops=1000,
            moved=1000,
        )(turned)
    with jax.named_scope("known"):
        known = coherence_chunk(spectra[0], nugget[0], decay[0], core, chip)
        known, high, low, yield_keep, yield_send = lax.optimization_barrier((known, high, low, yield_keep, yield_send))
        chunk = known - jnp.sum(parts, axis=0)
        chunk, yield_send = lax.optimization_barrier((chunk, yield_send))
        prior = yield_keep + swap(yield_send)
    with jax.named_scope("gather_first"):
        own = exchange(jnp.broadcast_to(chunk[None, :FIRST_ROWS], (CHIPS, FIRST_ROWS, BLK)))
        own, prior = lax.optimization_barrier((own, prior))
        other = swap(own)
    with jax.named_scope("gather_second"):
        rest, other = lax.optimization_barrier(
            (jnp.broadcast_to(chunk[None, FIRST_ROWS:], (CHIPS, SECOND_ROWS, BLK)), other)
        )
        own_rest = exchange(rest)
    with jax.named_scope("leading"):
        upper, inverse, left = call(
            leading_kernel,
            "leading",
            (f32(HALF - BLK, HALF), f32(3, BLK, BLK), f32(BLK, BLK)),
            [SMEM, VMEM, VMEM],
            [pltpu.VMEM((HALF, HALF), jnp.float32)],
            flops=20 * 10**9,
            moved=2 * 2**20,
        )(where, own, other)
    with jax.named_scope("gather_last"):
        own_rest, prior, left = lax.optimization_barrier((own_rest, prior, left))
        other_rest = swap(own_rest)
        prior_parts = exchange(prior.reshape(CHIPS, 32, 2 * SEEDS))
    with jax.named_scope("corner"):
        corner, corner_inverse = call(
            corner_kernel, "corner", (f32(BLK, BLK), f32(1, BLK, BLK)), [VMEM], flops=6 * 10**9, moved=2**17
        )(left)
    square = pltpu.VMEM((HALF, HALF), jnp.float32)
    with jax.named_scope("cross"):
        cross, work = call(
            cross_kernel,
            "cross",
            (f32(HALF, HALF),) * 2,
            [SMEM] + [VMEM] * 5,
            [square],
            flops=7 * 10**9,
            moved=4 * 2**20,
        )(where, own_rest, other_rest, upper, inverse, corner_inverse)
    with jax.named_scope("trailing"):
        amp = call(
            trailing_kernel,
            "trailing",
            f32(FREQS, 32, BLK),
            [SMEM] + [VMEM] * 4 + [HBM] * 2,
            [square] * 2
            + [pltpu.VMEM((4, BLK, BLK), jnp.float32), square]
            + [pltpu.VMEM((2 * SEEDS, WINDOW), jnp.bfloat16)] * 2
            + [pltpu.SemaphoreType.DMA((2,))],
            flops=25 * 10**9,
            moved=4 * 2**20,
            vmem=VMEM_LAST,
        )(where, work, upper, corner, cross, high, low)
    with jax.named_scope("amplitude"):
        amp = call(
            finish_kernel,
            "finish",
            f32(FREQS, 32, BLK),
            [VMEM, VMEM],
            [pltpu.VMEM((FREQS, 32, BLK), jnp.float32)],
            flops=10**8,
            moved=2 * 2**20,
        )(amp, prior_parts)
        amp = lax.all_to_all(amp, "freq", split_axis=0, concat_axis=0, tiled=True)
    with jax.named_scope("synthesis"):
        return call(synthesis_kernel, "synthesis", f32(64, 32, STEPS), [VMEM, VMEM], flops=10**8, moved=2 * 2**20)(
            amp, tables()
        )


def solution(mesh):
    chips = Mesh(mesh.devices.reshape(8, 4, 4, 2), ("freq", "row", "y", "core"))
    own = ("row", "y", "core")
    in_specs = (
        P("freq", own, None),
        P("freq", own, None),
        P("freq", None, None),
        P("freq", None),
        P("freq", None),
        P("freq"),
    )
    return jax.shard_map(shards, mesh=chips, in_specs=in_specs, out_specs=P("freq", own, None), check_vma=False)
```

```python
import math

import jax
import jax.numpy as jnp
import numpy as np
from jax import lax
from jax.experimental import pallas as pl
from jax.experimental.pallas import tpu as pltpu
from jax.sharding import Mesh, PartitionSpec as P

GRID = 96
NPHASE = 4096
STEPS = 256
PRIOR = 26624
FIRST_BIN = 64
WINDOW = 1024
HALF = 512
SEEDS = 512
FREQS = 8
BLK = 128
CHIPS = 16
VMEM_BYTES = 16 * 1024 * 1024
VMEM_LAST = 58 * 1024 * 1024
EXACT = lax.Precision.HIGHEST

cross_weight = 0.3

BLOCKS = [(i, j) for j in range(8) for i in range(j + 1)]
CHUNK = len(BLOCKS) * BLK // (2 * CHIPS)

SINE = [(-1.0) ** i / math.factorial(2 * i + 1) for i in range(7)]


def placed():
    half = len(BLOCKS) // 2
    for index, pair in enumerate(BLOCKS):
        runs = []
        at = 0
        while at < BLK:
            chip, inside = divmod(index % half * BLK + at, CHUNK)
            length = min(CHUNK - inside, BLK - at)
            runs.append((at, chip, inside, length))
            at += length
        yield pair, index // half, runs


def cosine(index):
    folded = jnp.abs(index - NPHASE // 2) - NPHASE // 4
    x = folded.astype(jnp.float32) * jnp.float32(2.0 * math.pi / NPHASE)
    y = x * x
    poly = jnp.full_like(x, SINE[-1])
    for c in SINE[-2::-1]:
        poly = poly * y + jnp.float32(c)
    return poly * x


def quarter_back(index):
    return (index + 3 * NPHASE // 4) & (NPHASE - 1)


def dot_t(a, b, precision=None):
    return lax.dot_general(a, b, (((0,), (0,)), ((), ())), preferred_element_type=jnp.float32, precision=precision)


def dot(a, b, precision=None):
    return jnp.dot(a, b, preferred_element_type=jnp.float32, precision=precision)


def schur_kernel(where_ref, cols_ref, keep_ref, send_ref, turned_ref):
    core = where_ref[0]
    spot = {pair: (half, runs) for pair, half, runs in placed()}
    turn(cols_ref, turned_ref)
    for group in range(4):
        product = dot(turned_ref[: 256 * (group + 1), :], cols_ref[:, 256 * group : 256 * (group + 1)])
        for j in (2 * group, 2 * group + 1):
            for i in range(j + 1):
                half, runs = spot[(i, j)]
                block = product[BLK * i : BLK * (i + 1), BLK * (j % 2) : BLK * (j % 2 + 1)]

                @pl.when(core == half)
                def _():
                    for at, chip, row, length in runs:
                        keep_ref[chip, row : row + length, :] = block[at : at + length, :]

                @pl.when(core != half)
                def _():
                    for at, chip, row, length in runs:
                        send_ref[chip, row : row + length, :] = block[at : at + length, :]


def turn(cols_ref, turned_ref):
    for i in range(8):
        turned_ref[BLK * i : BLK * (i + 1), :] = cols_ref[:, BLK * i : BLK * (i + 1)].T


def prior_kernel(where_ref, cols_ref, seeds_ref, keep_ref, send_ref, turned_ref):
    core = where_ref[0]
    turn(cols_ref, turned_ref)
    for piece in range(2):
        index = seeds_ref[:, 256 * piece : 256 * (piece + 1)]
        for at, phase in ((256 * piece, index), (SEEDS + 256 * piece, quarter_back(index))):
            product = dot(turned_ref[...], cosine(phase).astype(jnp.bfloat16))

            def store(half, target):
                for owner in range(half, 32, 2):
                    for upper in range(2):
                        row = 32 * (owner // 2) + 16 * upper
                        start = HALF * upper + 16 * owner
                        target[row : row + 16, at : at + 256] = product[start : start + 16, :]

            @pl.when(core == 0)
            def _():
                store(0, keep_ref)
                store(1, send_ref)

            @pl.when(core != 0)
            def _():
                store(1, keep_ref)
                store(0, send_ref)


def window_waves_kernel(seeds_ref, high_ref, low_ref):
    for piece in range(8):
        rows = slice(64 * piece, 64 * (piece + 1))
        lower = slice(SEEDS + 64 * piece, SEEDS + 64 * (piece + 1))
        index = seeds_ref[rows, :]
        for place, value in ((rows, cosine(index)), (lower, cosine(quarter_back(index)))):
            high = value.astype(jnp.bfloat16)
            high_ref[place, :] = high
            low_ref[place, :] = (value - high.astype(jnp.float32)).astype(jnp.bfloat16)


def bl(x, lane):
    return jnp.broadcast_to(x[:, lane : lane + 1], (8, BLK))


def bs(x, row):
    return jnp.broadcast_to(x[row : row + 1, :], (8, BLK))


def inverse_factor(rows):
    lane = lax.broadcasted_iota(jnp.int32, (8, BLK), 1)
    sub = lax.broadcasted_iota(jnp.int32, (8, BLK), 0)
    rows = list(rows)
    out = []
    cols = [bl(rows[0], k) for k in range(8)]
    for p in range(16):
        base = 8 * p
        inside = (lane >= base) & (lane < base + 8)
        here = rows[p]
        a = [[bs(cols[k], i) if k >= i else None for k in range(8)] for i in range(8)]
        scale = []
        for j in range(8):
            s = lax.rsqrt(a[j][j])
            scale.append(s)
            for k in range(j + 1, 8):
                a[j][k] = a[j][k] * s
            for i in range(j + 1, 8):
                for k in range(i, 8):
                    a[i][k] = a[i][k] - a[j][i] * a[j][k]

        def forward(r):
            r = list(r)
            for j in range(8):
                r[j] = r[j] * scale[j]
                for i in range(j + 1, 8):
                    r[i] = r[i] - a[j][i] * r[j]
            return r

        eye = jnp.where(lane - base == sub, 1.0, 0.0)
        mixed = jnp.where(inside, eye, here)
        u = forward([bs(mixed, i) for i in range(8)])
        done = u[0]
        for j in range(1, 8):
            done = jnp.where(sub == j, u[j], done)
        out.append(jnp.where(lane < base + 8, done, 0.0))
        if p == 15:
            break
        n = forward([bl(rows[p + 1], base + j) for j in range(8)])
        cols = []
        for k in range(8):
            t = [n[j] * bs(n[j], k) for j in range(8)]
            t = ((t[0] + t[1]) + (t[2] + t[3])) + ((t[4] + t[5]) + t[6]) + t[7]
            cols.append(bl(rows[p + 1], base + 8 + k) - t)
        t = [n[j] * u[j] for j in range(8)]
        t = (((t[0] + t[1]) + (t[2] + t[3])) + ((t[4] + t[5]) + t[6])) + t[7]
        rows[p + 1] = jnp.where(inside, 0.0, rows[p + 1]) - t
        if p == 14:
            continue
        w = [None] * 8
        for j in range(7, -1, -1):
            v = u[j]
            for k in range(j + 1, 8):
                v = v - a[j][k] * w[k]
            w[j] = v * scale[j]
        for r in range(p + 2, 16):
            v = jnp.where(inside, 0.0, rows[r])
            for j in range(8):
                v = v - bl(rows[r], base + j) * w[j]
            rows[r] = v
    return out


def factor(work_ref, upper_ref, inverse_ref):
    above = lax.broadcasted_iota(jnp.int32, (BLK, BLK), 0) <= lax.broadcasted_iota(jnp.int32, (BLK, BLK), 1)
    for k in range(8):
        top = BLK * k
        found = inverse_factor([work_ref[top + 8 * r : top + 8 * (r + 1), top : top + BLK] for r in range(16)])
        for r in range(16):
            inverse_ref[k, 8 * r : 8 * (r + 1), :] = found[r]
        row = dot(inverse_ref[k], work_ref[top : top + BLK, top:], EXACT)
        if k:
            upper_ref[top : top + BLK, :top] = jnp.zeros((BLK, top), jnp.float32)
        upper_ref[top : top + BLK, top : top + BLK] = jnp.where(above, row[:, :BLK], 0.0)
        if k < 7:
            upper_ref[top : top + BLK, top + BLK :] = row[:, BLK:]
        for i in range(k + 1, 8):
            work_ref[BLK * i : BLK * (i + 1), BLK * i :] -= dot_t(
                row[:, BLK * (i - k) : BLK * (i - k + 1)], row[:, BLK * (i - k) :], EXACT
            )


def factor_kernel(
    where_ref,
    own_ref,
    other_ref,
    high_ref,
    low_ref,
    out_ref,
    work_ref,
    upper_ref,
    inverse_ref,
    high_here,
    low_here,
    semaphores,
):
    fetches = [
        pltpu.make_async_copy(source, target, semaphores.at[i])
        for i, (source, target) in enumerate(((high_ref, high_here), (low_ref, low_here)))
    ]
    for fetch in fetches:
        fetch.start()
    core = where_ref[0]
    for (i, j), half, runs in placed():
        for at, chip, row, length in runs:
            span = slice(row, row + length)
            work_ref[BLK * i + at : BLK * i + at + length, BLK * j : BLK * (j + 1)] = jnp.where(
                core == half, own_ref[chip, span, :], other_ref[chip, span, :]
            )
    factor(work_ref, upper_ref, inverse_ref)
    for fetch in fetches:
        fetch.wait()
    amplitude(where_ref[1], upper_ref, high_here, low_here, out_ref)


def split(x):
    high = x.astype(jnp.bfloat16)
    return high, (x - high.astype(jnp.float32)).astype(jnp.bfloat16)


def amplitude(owner, upper_ref, high_ref, low_ref, out_ref):
    start = pl.multiple_of(owner // 8 * BLK, BLK)
    shift = owner % 8 * 16
    column = lax.broadcasted_iota(jnp.int32, (BLK, BLK), 0)
    wanted = lax.broadcasted_iota(jnp.int32, (BLK, BLK), 1) % 32
    pick_first = jnp.where((wanted < 16) & (column == shift + wanted), 1.0, 0.0).astype(jnp.bfloat16)
    pick_second = jnp.where((wanted >= 16) & (column == shift + wanted - 16), 1.0, 0.0).astype(jnp.bfloat16)
    first = split(upper_ref[:, pl.ds(start, BLK)])
    second = split(upper_ref[:, pl.ds(start + HALF, BLK)])
    mine = [
        (dot(first[part], pick_first) + dot(second[part], pick_second)).astype(jnp.bfloat16) for part in range(2)
    ]
    both = jnp.concatenate(mine, axis=1)
    for piece in range(8):
        rows = slice(BLK * piece, BLK * (piece + 1))
        wide = dot(high_ref[rows, :], both)
        fold(piece, wide[:, :BLK] + wide[:, BLK:] + dot(low_ref[rows, :], mine[0]), out_ref)


def fold(piece, amp, out_ref):
    group = lax.broadcasted_iota(jnp.int32, (16, BLK), 1) // 32
    for part in range(2):
        run = amp[64 * part : 64 * (part + 1), :]
        merged = run[:16]
        for s in range(1, 4):
            merged = jnp.where(group == s, run[16 * s : 16 * (s + 1)], merged)
        row = 16 * (piece // 4)
        out_ref[2 * (piece % 4) + part, row : row + 16, :] = merged


def finish_kernel(amp_ref, parts_ref, out_ref, total_ref):
    repeat = jnp.where(
        lax.broadcasted_iota(jnp.int32, (32, BLK), 1) % 32 == lax.broadcasted_iota(jnp.int32, (32, BLK), 0), 1.0, 0.0
    )
    for piece in range(8):
        lanes = slice(BLK * piece, BLK * (piece + 1))
        fold(piece, dot_t(jnp.sum(parts_ref[:, :, lanes], axis=0), repeat, EXACT), total_ref)
    out_ref[...] = amp_ref[...] + total_ref[...]


def synthesis_kernel(amp_ref, table_ref, out_ref):
    for s in range(16):
        lines = jnp.concatenate([amp_ref[:, s, :], amp_ref[:, 16 + s, :]], axis=0)
        series = dot_t(lines, table_ref[...], EXACT)
        for part in range(4):
            out_ref[16 * part + s] = series[32 * part : 32 * (part + 1), :]


SMEM = pl.BlockSpec(memory_space=pltpu.SMEM)
VMEM = pl.BlockSpec(memory_space=pltpu.VMEM)
HBM = pl.BlockSpec(memory_space=pltpu.HBM)


def call(kernel, name, outs, ins, scratch=(), flops=0, moved=0, vmem=VMEM_BYTES):
    return pl.pallas_call(
        kernel,
        out_shape=outs,
        in_specs=ins,
        out_specs=jax.tree.map(lambda _: VMEM, outs),
        scratch_shapes=list(scratch),
        compiler_params=pltpu.CompilerParams(vmem_limit_bytes=vmem),
        cost_estimate=pl.CostEstimate(flops=flops, bytes_accessed=moved, transcendentals=0),
        name=name,
    )


def f32(*shape):
    return jax.ShapeDtypeStruct(shape, jnp.float32)


def lookup(table, index):
    result = jnp.zeros_like(index)
    for at, value in enumerate(table):
        result = jnp.where(index == at, value, result)
    return result


def coherence_chunk(spectra, nugget, decay, core, chip):
    flat = (core * CHIPS + chip) * CHUNK + jnp.arange(CHUNK, dtype=jnp.int32)
    block = flat // BLK
    row_ids = lookup([i for i, _ in BLOCKS], block) * BLK + flat % BLK
    block_col = lookup([j for _, j in BLOCKS], block)
    col_ids = block_col[:, None] * BLK + jnp.arange(BLK, dtype=jnp.int32)[None, :]
    chosen = row_ids[:, None] == jnp.arange(WINDOW, dtype=jnp.int32)[None, :]
    row_spectra = jnp.sum(jnp.where(chosen, spectra[None, :], 0.0), axis=1)
    row_nugget = jnp.sum(jnp.where(chosen, nugget[None, :], 0.0), axis=1)
    by_block = spectra.reshape(8, BLK)
    col_spectra = jnp.zeros((CHUNK, BLK), jnp.float32)
    for j in range(8):
        col_spectra = jnp.where((block_col == j)[:, None], by_block[j][None, :], col_spectra)
    row_global = (PRIOR + row_ids)[:, None]
    col_global = PRIOR + col_ids
    row_points = row_global // 3
    col_points = col_global // 3
    across = (row_points % GRID - col_points % GRID).astype(jnp.float32)
    height = (row_points // GRID - col_points // GRID).astype(jnp.float32)
    distance = jnp.sqrt(across * across + height * height)
    coupling = jnp.where(row_global % 3 == col_global % 3, jnp.float32(1.0), jnp.float32(cross_weight))
    amplitude = jnp.sqrt(row_spectra[:, None] * col_spectra)
    diagonal = jnp.where(row_ids[:, None] == col_ids, row_nugget[:, None], jnp.float32(0.0))
    return coupling * amplitude * jnp.exp(-decay * distance) + diagonal


def tables():
    bins = FIRST_BIN + np.arange(FREQS)
    turns = (bins[:, None] * np.arange(STEPS)[None, :] % STEPS) * (2.0 * math.pi / STEPS)
    return jnp.asarray(np.concatenate([np.cos(turns), -np.sin(turns)], axis=0), jnp.float32)


CHIP_AXES = ("row", "y")


def exchange(x):
    return lax.all_to_all(x, CHIP_AXES, split_axis=0, concat_axis=0, tiled=True)


def swap(x):
    return lax.ppermute(x, "core", [(0, 1), (1, 0)])


def shards(prior_factor, prior_seeds, window_seeds, spectra, nugget, decay):
    cols = prior_factor[0]
    depth = cols.shape[0]
    core = lax.axis_index("core")
    chip = lax.axis_index(CHIP_AXES)
    owner = lax.axis_index(("row", "y", "core"))
    where = jnp.stack([core, owner]).astype(jnp.int32)

    with jax.named_scope("schur"):
        turned = pltpu.VMEM((WINDOW, depth), jnp.bfloat16)
        keep, send = call(
            schur_kernel,
            "schur",
            (f32(CHIPS, CHUNK, BLK),) * 2,
            [SMEM, VMEM],
            [turned],
            flops=10**9,
            moved=4 * 2**20,
        )(where, cols)
        received = swap(send)
    with jax.named_scope("reduce"):
        summed, seeds = lax.optimization_barrier((keep + received, prior_seeds[0]))
        parts = exchange(summed)
    with jax.named_scope("prior"):
        yield_keep, yield_send = call(
            prior_kernel,
            "prior",
            (f32(WINDOW // 2, 2 * SEEDS),) * 2,
            [SMEM, VMEM, VMEM],
            [turned],
            flops=1000,
            moved=1000,
        )(where, cols, seeds)
    with jax.named_scope("known"):
        known = coherence_chunk(spectra[0], nugget[0], decay[0], core, chip)
        known, yield_keep, yield_send = lax.optimization_barrier((known, yield_keep, yield_send))
        chunk = known - jnp.sum(parts, axis=0)
        chunk, yield_send, window_index = lax.optimization_barrier((chunk, yield_send, window_seeds[0]))
        prior = yield_keep + swap(yield_send)
    with jax.named_scope("gather"):
        own = exchange(jnp.broadcast_to(chunk[None], (CHIPS, CHUNK, BLK)))
    with jax.named_scope("window"):
        high, low = call(
            window_waves_kernel,
            "window_waves",
            (jax.ShapeDtypeStruct((2 * SEEDS, WINDOW), jnp.bfloat16),) * 2,
            [VMEM],
            flops=1000,
            moved=1000,
        )(window_index.T)
        own, prior, high, low = lax.optimization_barrier((own, prior, high, low))
        other = swap(own)
        prior_parts = exchange(prior.reshape(CHIPS, 32, 2 * SEEDS))
    with jax.named_scope("factor"):
        square = pltpu.VMEM((WINDOW, WINDOW), jnp.float32)
        waves = pltpu.VMEM((2 * SEEDS, WINDOW), jnp.bfloat16)
        amp = call(
            factor_kernel,
            "factor",
            f32(FREQS, 32, BLK),
            [SMEM] + [VMEM] * 2 + [HBM] * 2,
            [square, square, pltpu.VMEM((8, BLK, BLK), jnp.float32), waves, waves, pltpu.SemaphoreType.DMA((2,))],
            flops=60 * 10**9,
            moved=4 * 2**20,
            vmem=VMEM_LAST,
        )(where, own, other, high, low)
    with jax.named_scope("amplitude"):
        amp = call(
            finish_kernel,
            "finish",
            f32(FREQS, 32, BLK),
            [VMEM, VMEM],
            [pltpu.VMEM((FREQS, 32, BLK), jnp.float32)],
            flops=10**8,
            moved=2 * 2**20,
        )(amp, prior_parts)
        amp = lax.all_to_all(amp, "freq", split_axis=0, concat_axis=0, tiled=True)
    with jax.named_scope("synthesis"):
        return call(synthesis_kernel, "synthesis", f32(64, 32, STEPS), [VMEM, VMEM], flops=10**8, moved=2 * 2**20)(
            amp, tables()
        )


def solution(mesh):
    chips = Mesh(mesh.devices.reshape(8, 4, 4, 2), ("freq", "row", "y", "core"))
    own = ("row", "y", "core")
    in_specs = (
        P("freq", own, None),
        P("freq", own, None),
        P("freq", None, None),
        P("freq", None),
        P("freq", None),
        P("freq"),
    )
    return jax.shard_map(shards, mesh=chips, in_specs=in_specs, out_specs=P("freq", own, None), check_vma=False)
```

```python
import math

import jax
import jax.numpy as jnp
import numpy as np
from jax import lax
from jax.experimental import pallas as pl
from jax.experimental.pallas import tpu as pltpu
from jax.sharding import Mesh, PartitionSpec as P

GRID = 96
NPHASE = 4096
STEPS = 256
PRIOR = 26624
FIRST_BIN = 64
WINDOW = 1024
HALF = 512
SEEDS = 512
FREQS = 8
BLK = 128
CHIPS = 16
VMEM_BYTES = 16 * 1024 * 1024
VMEM_LAST = 58 * 1024 * 1024
EXACT = lax.Precision.HIGHEST

cross_weight = 0.3

BLOCKS = [(i, j) for j in range(8) for i in range(j + 1)]
CHUNK = len(BLOCKS) * BLK // (2 * CHIPS)

SINE = [(-1.0) ** i / math.factorial(2 * i + 1) for i in range(7)]


def placed():
    half = len(BLOCKS) // 2
    for index, pair in enumerate(BLOCKS):
        runs = []
        at = 0
        while at < BLK:
            chip, inside = divmod(index % half * BLK + at, CHUNK)
            length = min(CHUNK - inside, BLK - at)
            runs.append((at, chip, inside, length))
            at += length
        yield pair, index // half, runs


def cosine(index):
    folded = jnp.abs(index - NPHASE // 2) - NPHASE // 4
    x = folded.astype(jnp.float32) * jnp.float32(2.0 * math.pi / NPHASE)
    y = x * x
    poly = jnp.full_like(x, SINE[-1])
    for c in SINE[-2::-1]:
        poly = poly * y + jnp.float32(c)
    return poly * x


def quarter_back(index):
    return (index + 3 * NPHASE // 4) & (NPHASE - 1)


def dot_t(a, b, precision=None):
    return lax.dot_general(a, b, (((0,), (0,)), ((), ())), preferred_element_type=jnp.float32, precision=precision)


def dot(a, b, precision=None):
    return jnp.dot(a, b, preferred_element_type=jnp.float32, precision=precision)


def schur_kernel(where_ref, cols_ref, keep_ref, send_ref, turned_ref):
    core = where_ref[0]
    spot = {pair: (half, runs) for pair, half, runs in placed()}
    turn(cols_ref, turned_ref)
    for group in range(4):
        product = dot(turned_ref[: 256 * (group + 1), :], cols_ref[:, 256 * group : 256 * (group + 1)])
        for j in (2 * group, 2 * group + 1):
            for i in range(j + 1):
                half, runs = spot[(i, j)]
                block = product[BLK * i : BLK * (i + 1), BLK * (j % 2) : BLK * (j % 2 + 1)]

                @pl.when(core == half)
                def _():
                    for at, chip, row, length in runs:
                        keep_ref[chip, row : row + length, :] = block[at : at + length, :]

                @pl.when(core != half)
                def _():
                    for at, chip, row, length in runs:
                        send_ref[chip, row : row + length, :] = block[at : at + length, :]


def turn(cols_ref, turned_ref):
    for i in range(8):
        turned_ref[BLK * i : BLK * (i + 1), :] = cols_ref[:, BLK * i : BLK * (i + 1)].T


def prior_kernel(where_ref, cols_ref, seeds_ref, keep_ref, send_ref, turned_ref):
    core = where_ref[0]
    turn(cols_ref, turned_ref)
    for piece in range(2):
        index = seeds_ref[:, 256 * piece : 256 * (piece + 1)]
        for at, phase in ((256 * piece, index), (SEEDS + 256 * piece, quarter_back(index))):
            product = dot(turned_ref[...], cosine(phase).astype(jnp.bfloat16))

            def store(half, target):
                for owner in range(half, 32, 2):
                    for upper in range(2):
                        row = 32 * (owner // 2) + 16 * upper
                        start = HALF * upper + 16 * owner
                        target[row : row + 16, at : at + 256] = product[start : start + 16, :]

            @pl.when(core == 0)
            def _():
                store(0, keep_ref)
                store(1, send_ref)

            @pl.when(core != 0)
            def _():
                store(1, keep_ref)
                store(0, send_ref)


def window_waves_kernel(seeds_ref, high_ref, low_ref):
    for piece in range(8):
        rows = slice(64 * piece, 64 * (piece + 1))
        lower = slice(SEEDS + 64 * piece, SEEDS + 64 * (piece + 1))
        index = seeds_ref[rows, :]
        for place, value in ((rows, cosine(index)), (lower, cosine(quarter_back(index)))):
            high = value.astype(jnp.bfloat16)
            high_ref[place, :] = high
            low_ref[place, :] = (value - high.astype(jnp.float32)).astype(jnp.bfloat16)


def bl(x, lane):
    return jnp.broadcast_to(x[:, lane : lane + 1], (8, BLK))


def bs(x, row):
    return jnp.broadcast_to(x[row : row + 1, :], (8, BLK))


def inverse_factor(rows):
    lane = lax.broadcasted_iota(jnp.int32, (8, BLK), 1)
    sub = lax.broadcasted_iota(jnp.int32, (8, BLK), 0)
    rows = list(rows)
    out = []
    cols = [bl(rows[0], k) for k in range(8)]
    for p in range(16):
        base = 8 * p
        inside = (lane >= base) & (lane < base + 8)
        here = rows[p]
        a = [[bs(cols[k], i) if k >= i else None for k in range(8)] for i in range(8)]
        scale = []
        for j in range(8):
            s = lax.rsqrt(a[j][j])
            scale.append(s)
            for k in range(j + 1, 8):
                a[j][k] = a[j][k] * s
            for i in range(j + 1, 8):
                for k in range(i, 8):
                    a[i][k] = a[i][k] - a[j][i] * a[j][k]

        def forward(r):
            r = list(r)
            for j in range(8):
                r[j] = r[j] * scale[j]
                for i in range(j + 1, 8):
                    r[i] = r[i] - a[j][i] * r[j]
            return r

        eye = jnp.where(lane - base == sub, 1.0, 0.0)
        mixed = jnp.where(inside, eye, here)
        u = forward([bs(mixed, i) for i in range(8)])
        done = u[0]
        for j in range(1, 8):
            done = jnp.where(sub == j, u[j], done)
        out.append(jnp.where(lane < base + 8, done, 0.0))
        if p == 15:
            break
        n = forward([bl(rows[p + 1], base + j) for j in range(8)])
        cols = []
        for k in range(8):
            t = [n[j] * bs(n[j], k) for j in range(8)]
            t = ((t[0] + t[1]) + (t[2] + t[3])) + ((t[4] + t[5]) + t[6]) + t[7]
            cols.append(bl(rows[p + 1], base + 8 + k) - t)
        t = [n[j] * u[j] for j in range(8)]
        t = (((t[0] + t[1]) + (t[2] + t[3])) + ((t[4] + t[5]) + t[6])) + t[7]
        rows[p + 1] = jnp.where(inside, 0.0, rows[p + 1]) - t
        if p == 14:
            continue
        w = [None] * 8
        for j in range(7, -1, -1):
            v = u[j]
            for k in range(j + 1, 8):
                v = v - a[j][k] * w[k]
            w[j] = v * scale[j]
        for r in range(p + 2, 16):
            v = jnp.where(inside, 0.0, rows[r])
            for j in range(8):
                v = v - bl(rows[r], base + j) * w[j]
            rows[r] = v
    return out


def factor(work_ref, upper_ref, inverse_ref):
    above = lax.broadcasted_iota(jnp.int32, (BLK, BLK), 0) <= lax.broadcasted_iota(jnp.int32, (BLK, BLK), 1)
    for k in range(8):
        top = BLK * k
        found = inverse_factor([work_ref[top + 8 * r : top + 8 * (r + 1), top : top + BLK] for r in range(16)])
        for r in range(16):
            inverse_ref[k, 8 * r : 8 * (r + 1), :] = found[r]
        row = dot(inverse_ref[k], work_ref[top : top + BLK, top:], EXACT)
        if k:
            upper_ref[top : top + BLK, :top] = jnp.zeros((BLK, top), jnp.float32)
        upper_ref[top : top + BLK, top : top + BLK] = jnp.where(above, row[:, :BLK], 0.0)
        if k < 7:
            upper_ref[top : top + BLK, top + BLK :] = row[:, BLK:]
        for i in range(k + 1, 8):
            work_ref[BLK * i : BLK * (i + 1), BLK * i :] -= dot_t(
                row[:, BLK * (i - k) : BLK * (i - k + 1)], row[:, BLK * (i - k) :], EXACT
            )


def factor_kernel(
    where_ref,
    own_ref,
    other_ref,
    high_ref,
    low_ref,
    out_ref,
    work_ref,
    upper_ref,
    inverse_ref,
    high_here,
    low_here,
    semaphores,
):
    fetches = [
        pltpu.make_async_copy(source, target, semaphores.at[i])
        for i, (source, target) in enumerate(((high_ref, high_here), (low_ref, low_here)))
    ]
    for fetch in fetches:
        fetch.start()
    core = where_ref[0]
    for (i, j), half, runs in placed():
        for at, chip, row, length in runs:
            span = slice(row, row + length)
            work_ref[BLK * i + at : BLK * i + at + length, BLK * j : BLK * (j + 1)] = jnp.where(
                core == half, own_ref[chip, span, :], other_ref[chip, span, :]
            )
    factor(work_ref, upper_ref, inverse_ref)
    for fetch in fetches:
        fetch.wait()
    amplitude(where_ref[1], upper_ref, high_here, low_here, out_ref)


def split(x):
    high = x.astype(jnp.bfloat16)
    return high, (x - high.astype(jnp.float32)).astype(jnp.bfloat16)


def amplitude(owner, upper_ref, high_ref, low_ref, out_ref):
    start = pl.multiple_of(owner // 8 * BLK, BLK)
    shift = owner % 8 * 16
    column = lax.broadcasted_iota(jnp.int32, (BLK, BLK), 0)
    wanted = lax.broadcasted_iota(jnp.int32, (BLK, BLK), 1) % 32
    pick_first = jnp.where((wanted < 16) & (column == shift + wanted), 1.0, 0.0).astype(jnp.bfloat16)
    pick_second = jnp.where((wanted >= 16) & (column == shift + wanted - 16), 1.0, 0.0).astype(jnp.bfloat16)
    first = split(upper_ref[:, pl.ds(start, BLK)])
    second = split(upper_ref[:, pl.ds(start + HALF, BLK)])
    mine = [
        (dot(first[part], pick_first) + dot(second[part], pick_second)).astype(jnp.bfloat16) for part in range(2)
    ]
    both = jnp.concatenate(mine, axis=1)
    for piece in range(8):
        rows = slice(BLK * piece, BLK * (piece + 1))
        wide = dot(high_ref[rows, :], both)
        fold(piece, wide[:, :BLK] + wide[:, BLK:] + dot(low_ref[rows, :], mine[0]), out_ref)


def fold(piece, amp, out_ref):
    group = lax.broadcasted_iota(jnp.int32, (16, BLK), 1) // 32
    for part in range(2):
        run = amp[64 * part : 64 * (part + 1), :]
        merged = run[:16]
        for s in range(1, 4):
            merged = jnp.where(group == s, run[16 * s : 16 * (s + 1)], merged)
        row = 16 * (piece // 4)
        out_ref[2 * (piece % 4) + part, row : row + 16, :] = merged


def finish_kernel(amp_ref, parts_ref, out_ref, total_ref):
    repeat = jnp.where(
        lax.broadcasted_iota(jnp.int32, (32, BLK), 1) % 32 == lax.broadcasted_iota(jnp.int32, (32, BLK), 0), 1.0, 0.0
    )
    for piece in range(8):
        lanes = slice(BLK * piece, BLK * (piece + 1))
        fold(piece, dot_t(jnp.sum(parts_ref[:, :, lanes], axis=0), repeat, EXACT), total_ref)
    out_ref[...] = amp_ref[...] + total_ref[...]


def synthesis_kernel(amp_ref, table_ref, out_ref):
    for s in range(16):
        lines = jnp.concatenate([amp_ref[:, s, :], amp_ref[:, 16 + s, :]], axis=0)
        series = dot_t(lines, table_ref[...], EXACT)
        for part in range(4):
            out_ref[16 * part + s] = series[32 * part : 32 * (part + 1), :]


SMEM = pl.BlockSpec(memory_space=pltpu.SMEM)
VMEM = pl.BlockSpec(memory_space=pltpu.VMEM)
HBM = pl.BlockSpec(memory_space=pltpu.HBM)


def call(kernel, name, outs, ins, scratch=(), flops=0, moved=0, vmem=VMEM_BYTES):
    return pl.pallas_call(
        kernel,
        out_shape=outs,
        in_specs=ins,
        out_specs=jax.tree.map(lambda _: VMEM, outs),
        scratch_shapes=list(scratch),
        compiler_params=pltpu.CompilerParams(vmem_limit_bytes=vmem),
        cost_estimate=pl.CostEstimate(flops=flops, bytes_accessed=moved, transcendentals=0),
        name=name,
    )


def f32(*shape):
    return jax.ShapeDtypeStruct(shape, jnp.float32)


def lookup(table, index):
    result = jnp.zeros_like(index)
    for at, value in enumerate(table):
        result = jnp.where(index == at, value, result)
    return result


def coherence_chunk(spectra, nugget, decay, core, chip):
    flat = (core * CHIPS + chip) * CHUNK + jnp.arange(CHUNK, dtype=jnp.int32)
    block = flat // BLK
    row_ids = lookup([i for i, _ in BLOCKS], block) * BLK + flat % BLK
    block_col = lookup([j for _, j in BLOCKS], block)
    col_ids = block_col[:, None] * BLK + jnp.arange(BLK, dtype=jnp.int32)[None, :]
    chosen = row_ids[:, None] == jnp.arange(WINDOW, dtype=jnp.int32)[None, :]
    row_spectra = jnp.sum(jnp.where(chosen, spectra[None, :], 0.0), axis=1)
    row_nugget = jnp.sum(jnp.where(chosen, nugget[None, :], 0.0), axis=1)
    by_block = spectra.reshape(8, BLK)
    col_spectra = jnp.zeros((CHUNK, BLK), jnp.float32)
    for j in range(8):
        col_spectra = jnp.where((block_col == j)[:, None], by_block[j][None, :], col_spectra)
    row_global = (PRIOR + row_ids)[:, None]
    col_global = PRIOR + col_ids
    row_points = row_global // 3
    col_points = col_global // 3
    across = (row_points % GRID - col_points % GRID).astype(jnp.float32)
    height = (row_points // GRID - col_points // GRID).astype(jnp.float32)
    distance = jnp.sqrt(across * across + height * height)
    coupling = jnp.where(row_global % 3 == col_global % 3, jnp.float32(1.0), jnp.float32(cross_weight))
    amplitude = jnp.sqrt(row_spectra[:, None] * col_spectra)
    diagonal = jnp.where(row_ids[:, None] == col_ids, row_nugget[:, None], jnp.float32(0.0))
    return coupling * amplitude * jnp.exp(-decay * distance) + diagonal


def tables():
    bins = FIRST_BIN + np.arange(FREQS)
    turns = (bins[:, None] * np.arange(STEPS)[None, :] % STEPS) * (2.0 * math.pi / STEPS)
    return jnp.asarray(np.concatenate([np.cos(turns), -np.sin(turns)], axis=0), jnp.float32)


CHIP_AXES = ("row", "y")


def exchange(x):
    return lax.all_to_all(x, CHIP_AXES, split_axis=0, concat_axis=0, tiled=True)


def swap(x):
    return lax.ppermute(x, "core", [(0, 1), (1, 0)])


def shards(prior_factor, prior_seeds, window_seeds, spectra, nugget, decay):
    cols = prior_factor[0]
    depth = cols.shape[0]
    core = lax.axis_index("core")
    chip = lax.axis_index(CHIP_AXES)
    owner = lax.axis_index(("row", "y", "core"))
    where = jnp.stack([core, owner]).astype(jnp.int32)

    with jax.named_scope("schur"):
        turned = pltpu.VMEM((WINDOW, depth), jnp.bfloat16)
        keep, send = call(
            schur_kernel,
            "schur",
            (f32(CHIPS, CHUNK, BLK),) * 2,
            [SMEM, VMEM],
            [turned],
            flops=10**9,
            moved=4 * 2**20,
        )(where, cols)
        received = swap(send)
    with jax.named_scope("reduce"):
        summed, seeds = lax.optimization_barrier((keep + received, prior_seeds[0]))
        parts = exchange(summed)
    with jax.named_scope("prior"):
        yield_keep, yield_send = call(
            prior_kernel,
            "prior",
            (f32(WINDOW // 2, 2 * SEEDS),) * 2,
            [SMEM, VMEM, VMEM],
            [turned],
            flops=1000,
            moved=1000,
        )(where, cols, seeds)
    with jax.named_scope("known"):
        known = coherence_chunk(spectra[0], nugget[0], decay[0], core, chip)
        known, yield_keep, yield_send = lax.optimization_barrier((known, yield_keep, yield_send))
        yield_received = swap(yield_send)
        chunk = known - jnp.sum(parts, axis=0)
        chunk, yield_keep, window_index = lax.optimization_barrier((chunk, yield_keep, window_seeds[0]))
        prior = yield_keep + yield_received
    with jax.named_scope("gather"):
        own = exchange(jnp.broadcast_to(chunk[None], (CHIPS, CHUNK, BLK)))
    with jax.named_scope("window"):
        high, low = call(
            window_waves_kernel,
            "window_waves",
            (jax.ShapeDtypeStruct((2 * SEEDS, WINDOW), jnp.bfloat16),) * 2,
            [VMEM],
            flops=1000,
            moved=1000,
        )(window_index.T)
        own, prior, high, low = lax.optimization_barrier((own, prior, high, low))
        other = swap(own)
        prior_parts = exchange(prior.reshape(CHIPS, 32, 2 * SEEDS))
    with jax.named_scope("factor"):
        square = pltpu.VMEM((WINDOW, WINDOW), jnp.float32)
        waves = pltpu.VMEM((2 * SEEDS, WINDOW), jnp.bfloat16)
        amp = call(
            factor_kernel,
            "factor",
            f32(FREQS, 32, BLK),
            [SMEM] + [VMEM] * 2 + [HBM] * 2,
            [square, square, pltpu.VMEM((8, BLK, BLK), jnp.float32), waves, waves, pltpu.SemaphoreType.DMA((2,))],
            flops=60 * 10**9,
            moved=4 * 2**20,
            vmem=VMEM_LAST,
        )(where, own, other, high, low)
    with jax.named_scope("amplitude"):
        amp = call(
            finish_kernel,
            "finish",
            f32(FREQS, 32, BLK),
            [VMEM, VMEM],
            [pltpu.VMEM((FREQS, 32, BLK), jnp.float32)],
            flops=10**8,
            moved=2 * 2**20,
        )(amp, prior_parts)
        amp = lax.all_to_all(amp, "freq", split_axis=0, concat_axis=0, tiled=True)
    with jax.named_scope("synthesis"):
        return call(synthesis_kernel, "synthesis", f32(64, 32, STEPS), [VMEM, VMEM], flops=10**8, moved=2 * 2**20)(
            amp, tables()
        )


def solution(mesh):
    chips = Mesh(mesh.devices.reshape(8, 4, 4, 2), ("freq", "row", "y", "core"))
    own = ("row", "y", "core")
    in_specs = (
        P("freq", own, None),
        P("freq", own, None),
        P("freq", None, None),
        P("freq", None),
        P("freq", None),
        P("freq"),
    )
    return jax.shard_map(shards, mesh=chips, in_specs=in_specs, out_specs=P("freq", own, None), check_vma=False)
```

```python
import math

import jax
import jax.numpy as jnp
import numpy as np
from jax import lax
from jax.experimental import pallas as pl
from jax.experimental.pallas import tpu as pltpu
from jax.sharding import Mesh, PartitionSpec as P

GRID = 96
NPHASE = 4096
STEPS = 256
PRIOR = 26624
FIRST_BIN = 64
WINDOW = 1024
HALF = 512
SEEDS = 512
FREQS = 8
BLK = 128
CHIPS = 16
VMEM_BYTES = 16 * 1024 * 1024
VMEM_LAST = 58 * 1024 * 1024
EXACT = lax.Precision.HIGHEST

cross_weight = 0.3

BLOCKS = [(i, j) for j in range(8) for i in range(j + 1)]
CHUNK = len(BLOCKS) * BLK // (2 * CHIPS)

SINE = [(-1.0) ** i / math.factorial(2 * i + 1) for i in range(7)]


def placed():
    half = len(BLOCKS) // 2
    for index, pair in enumerate(BLOCKS):
        runs = []
        at = 0
        while at < BLK:
            chip, inside = divmod(index % half * BLK + at, CHUNK)
            length = min(CHUNK - inside, BLK - at)
            runs.append((at, chip, inside, length))
            at += length
        yield pair, index // half, runs


def cosine(index):
    folded = jnp.abs(index - NPHASE // 2) - NPHASE // 4
    x = folded.astype(jnp.float32) * jnp.float32(2.0 * math.pi / NPHASE)
    y = x * x
    poly = jnp.full_like(x, SINE[-1])
    for c in SINE[-2::-1]:
        poly = poly * y + jnp.float32(c)
    return poly * x


def quarter_back(index):
    return (index + 3 * NPHASE // 4) & (NPHASE - 1)


def dot_t(a, b, precision=None):
    return lax.dot_general(a, b, (((0,), (0,)), ((), ())), preferred_element_type=jnp.float32, precision=precision)


def dot(a, b, precision=None):
    return jnp.dot(a, b, preferred_element_type=jnp.float32, precision=precision)


def schur_kernel(where_ref, cols_ref, keep_ref, send_ref, turned_ref):
    core = where_ref[0]
    spot = {pair: (half, runs) for pair, half, runs in placed()}
    turn(cols_ref, turned_ref)
    for group in range(4):
        product = dot(turned_ref[: 256 * (group + 1), :], cols_ref[:, 256 * group : 256 * (group + 1)])
        for j in (2 * group, 2 * group + 1):
            for i in range(j + 1):
                half, runs = spot[(i, j)]
                block = product[BLK * i : BLK * (i + 1), BLK * (j % 2) : BLK * (j % 2 + 1)]

                @pl.when(core == half)
                def _():
                    for at, chip, row, length in runs:
                        keep_ref[chip, row : row + length, :] = block[at : at + length, :]

                @pl.when(core != half)
                def _():
                    for at, chip, row, length in runs:
                        send_ref[chip, row : row + length, :] = block[at : at + length, :]


def turn(cols_ref, turned_ref):
    for i in range(8):
        turned_ref[BLK * i : BLK * (i + 1), :] = cols_ref[:, BLK * i : BLK * (i + 1)].T


def prior_kernel(where_ref, cols_ref, seeds_ref, keep_ref, send_ref, turned_ref):
    core = where_ref[0]
    turn(cols_ref, turned_ref)
    for piece in range(2):
        index = seeds_ref[:, 256 * piece : 256 * (piece + 1)]
        for at, phase in ((256 * piece, index), (SEEDS + 256 * piece, quarter_back(index))):
            product = dot(turned_ref[...], cosine(phase).astype(jnp.bfloat16))

            def store(half, target):
                for owner in range(half, 32, 2):
                    for upper in range(2):
                        row = 32 * (owner // 2) + 16 * upper
                        start = HALF * upper + 16 * owner
                        target[row : row + 16, at : at + 256] = product[start : start + 16, :]

            @pl.when(core == 0)
            def _():
                store(0, keep_ref)
                store(1, send_ref)

            @pl.when(core != 0)
            def _():
                store(1, keep_ref)
                store(0, send_ref)


def window_waves_kernel(seeds_ref, high_ref, low_ref):
    for piece in range(8):
        rows = slice(64 * piece, 64 * (piece + 1))
        lower = slice(SEEDS + 64 * piece, SEEDS + 64 * (piece + 1))
        index = seeds_ref[rows, :]
        for place, value in ((rows, cosine(index)), (lower, cosine(quarter_back(index)))):
            high = value.astype(jnp.bfloat16)
            high_ref[place, :] = high
            low_ref[place, :] = (value - high.astype(jnp.float32)).astype(jnp.bfloat16)


def bl(x, lane):
    return jnp.broadcast_to(x[:, lane : lane + 1], (8, BLK))


def bs(x, row):
    return jnp.broadcast_to(x[row : row + 1, :], (8, BLK))


def inverse_factor(rows):
    lane = lax.broadcasted_iota(jnp.int32, (8, BLK), 1)
    sub = lax.broadcasted_iota(jnp.int32, (8, BLK), 0)
    rows = list(rows)
    out = []
    cols = [bl(rows[0], k) for k in range(8)]
    for p in range(16):
        base = 8 * p
        inside = (lane >= base) & (lane < base + 8)
        here = rows[p]
        a = [[bs(cols[k], i) if k >= i else None for k in range(8)] for i in range(8)]
        scale = []
        for j in range(8):
            s = lax.rsqrt(a[j][j])
            scale.append(s)
            for k in range(j + 1, 8):
                a[j][k] = a[j][k] * s
            for i in range(j + 1, 8):
                for k in range(i, 8):
                    a[i][k] = a[i][k] - a[j][i] * a[j][k]

        def forward(r):
            r = list(r)
            for j in range(8):
                r[j] = r[j] * scale[j]
                for i in range(j + 1, 8):
                    r[i] = r[i] - a[j][i] * r[j]
            return r

        eye = jnp.where(lane - base == sub, 1.0, 0.0)
        mixed = jnp.where(inside, eye, here)
        u = forward([bs(mixed, i) for i in range(8)])
        done = u[0]
        for j in range(1, 8):
            done = jnp.where(sub == j, u[j], done)
        out.append(jnp.where(lane < base + 8, done, 0.0))
        if p == 15:
            break
        n = forward([bl(rows[p + 1], base + j) for j in range(8)])
        cols = []
        for k in range(8):
            t = [n[j] * bs(n[j], k) for j in range(8)]
            t = ((t[0] + t[1]) + (t[2] + t[3])) + ((t[4] + t[5]) + t[6]) + t[7]
            cols.append(bl(rows[p + 1], base + 8 + k) - t)
        t = [n[j] * u[j] for j in range(8)]
        t = (((t[0] + t[1]) + (t[2] + t[3])) + ((t[4] + t[5]) + t[6])) + t[7]
        rows[p + 1] = jnp.where(inside, 0.0, rows[p + 1]) - t
        if p == 14:
            continue
        w = [None] * 8
        for j in range(7, -1, -1):
            v = u[j]
            for k in range(j + 1, 8):
                v = v - a[j][k] * w[k]
            w[j] = v * scale[j]
        for r in range(p + 2, 16):
            v = jnp.where(inside, 0.0, rows[r])
            for j in range(8):
                v = v - bl(rows[r], base + j) * w[j]
            rows[r] = v
    return out


def factor(work_ref, upper_ref, inverse_ref):
    above = lax.broadcasted_iota(jnp.int32, (BLK, BLK), 0) <= lax.broadcasted_iota(jnp.int32, (BLK, BLK), 1)
    for k in range(8):
        top = BLK * k
        found = inverse_factor([work_ref[top + 8 * r : top + 8 * (r + 1), top : top + BLK] for r in range(16)])
        for r in range(16):
            inverse_ref[k, 8 * r : 8 * (r + 1), :] = found[r]
        row = dot(inverse_ref[k], work_ref[top : top + BLK, top:], EXACT)
        if k:
            upper_ref[top : top + BLK, :top] = jnp.zeros((BLK, top), jnp.float32)
        upper_ref[top : top + BLK, top : top + BLK] = jnp.where(above, row[:, :BLK], 0.0)
        if k < 7:
            upper_ref[top : top + BLK, top + BLK :] = row[:, BLK:]
        for i in range(k + 1, 8):
            work_ref[BLK * i : BLK * (i + 1), BLK * i :] -= dot_t(
                row[:, BLK * (i - k) : BLK * (i - k + 1)], row[:, BLK * (i - k) :], EXACT
            )


def factor_kernel(
    where_ref,
    own_ref,
    other_ref,
    high_ref,
    low_ref,
    out_ref,
    work_ref,
    upper_ref,
    inverse_ref,
    high_here,
    low_here,
    semaphores,
):
    fetches = [
        pltpu.make_async_copy(source, target, semaphores.at[i])
        for i, (source, target) in enumerate(((high_ref, high_here), (low_ref, low_here)))
    ]
    for fetch in fetches:
        fetch.start()
    core = where_ref[0]
    for (i, j), half, runs in placed():
        for at, chip, row, length in runs:
            span = slice(row, row + length)
            work_ref[BLK * i + at : BLK * i + at + length, BLK * j : BLK * (j + 1)] = jnp.where(
                core == half, own_ref[chip, span, :], other_ref[chip, span, :]
            )
    factor(work_ref, upper_ref, inverse_ref)
    for fetch in fetches:
        fetch.wait()
    amplitude(where_ref[1], upper_ref, high_here, low_here, out_ref)


def split(x):
    high = x.astype(jnp.bfloat16)
    return high, (x - high.astype(jnp.float32)).astype(jnp.bfloat16)


def amplitude(owner, upper_ref, high_ref, low_ref, out_ref):
    start = pl.multiple_of(owner // 8 * BLK, BLK)
    shift = owner % 8 * 16
    column = lax.broadcasted_iota(jnp.int32, (BLK, BLK), 0)
    wanted = lax.broadcasted_iota(jnp.int32, (BLK, BLK), 1) % 32
    pick_first = jnp.where((wanted < 16) & (column == shift + wanted), 1.0, 0.0).astype(jnp.bfloat16)
    pick_second = jnp.where((wanted >= 16) & (column == shift + wanted - 16), 1.0, 0.0).astype(jnp.bfloat16)
    first = split(upper_ref[:, pl.ds(start, BLK)])
    second = split(upper_ref[:, pl.ds(start + HALF, BLK)])
    mine = [
        (dot(first[part], pick_first) + dot(second[part], pick_second)).astype(jnp.bfloat16) for part in range(2)
    ]
    both = jnp.concatenate(mine, axis=1)
    for piece in range(8):
        rows = slice(BLK * piece, BLK * (piece + 1))
        wide = dot(high_ref[rows, :], both)
        fold(piece, wide[:, :BLK] + wide[:, BLK:] + dot(low_ref[rows, :], mine[0]), out_ref)


def fold(piece, amp, out_ref):
    group = lax.broadcasted_iota(jnp.int32, (16, BLK), 1) // 32
    for part in range(2):
        run = amp[64 * part : 64 * (part + 1), :]
        merged = run[:16]
        for s in range(1, 4):
            merged = jnp.where(group == s, run[16 * s : 16 * (s + 1)], merged)
        row = 16 * (piece // 4)
        out_ref[2 * (piece % 4) + part, row : row + 16, :] = merged


def finish_kernel(amp_ref, parts_ref, out_ref, total_ref):
    repeat = jnp.where(
        lax.broadcasted_iota(jnp.int32, (32, BLK), 1) % 32 == lax.broadcasted_iota(jnp.int32, (32, BLK), 0), 1.0, 0.0
    )
    for piece in range(8):
        lanes = slice(BLK * piece, BLK * (piece + 1))
        fold(piece, dot_t(jnp.sum(parts_ref[:, :, lanes], axis=0), repeat, EXACT), total_ref)
    out_ref[...] = amp_ref[...] + total_ref[...]


def synthesis_kernel(amp_ref, table_ref, out_ref):
    for s in range(8):
        high, low = split(jnp.concatenate([amp_ref[:, 0, s, :], amp_ref[:, 1, s, :]], axis=0))
        series = dot_t(jnp.concatenate([high, low, high], axis=0), table_ref[...])
        for part in range(4):
            out_ref[part, s] = series[32 * part : 32 * (part + 1), :]


SMEM = pl.BlockSpec(memory_space=pltpu.SMEM)
VMEM = pl.BlockSpec(memory_space=pltpu.VMEM)
HBM = pl.BlockSpec(memory_space=pltpu.HBM)


def call(kernel, name, outs, ins, scratch=(), flops=0, moved=0, vmem=VMEM_BYTES):
    return pl.pallas_call(
        kernel,
        out_shape=outs,
        in_specs=ins,
        out_specs=jax.tree.map(lambda _: VMEM, outs),
        scratch_shapes=list(scratch),
        compiler_params=pltpu.CompilerParams(vmem_limit_bytes=vmem),
        cost_estimate=pl.CostEstimate(flops=flops, bytes_accessed=moved, transcendentals=0),
        name=name,
    )


def f32(*shape):
    return jax.ShapeDtypeStruct(shape, jnp.float32)


def lookup(table, index):
    result = jnp.zeros_like(index)
    for at, value in enumerate(table):
        result = jnp.where(index == at, value, result)
    return result


def coherence_chunk(spectra, nugget, decay, core, chip):
    flat = (core * CHIPS + chip) * CHUNK + jnp.arange(CHUNK, dtype=jnp.int32)
    block = flat // BLK
    row_ids = lookup([i for i, _ in BLOCKS], block) * BLK + flat % BLK
    block_col = lookup([j for _, j in BLOCKS], block)
    col_ids = block_col[:, None] * BLK + jnp.arange(BLK, dtype=jnp.int32)[None, :]
    chosen = row_ids[:, None] == jnp.arange(WINDOW, dtype=jnp.int32)[None, :]
    row_spectra = jnp.sum(jnp.where(chosen, spectra[None, :], 0.0), axis=1)
    row_nugget = jnp.sum(jnp.where(chosen, nugget[None, :], 0.0), axis=1)
    by_block = spectra.reshape(8, BLK)
    col_spectra = jnp.zeros((CHUNK, BLK), jnp.float32)
    for j in range(8):
        col_spectra = jnp.where((block_col == j)[:, None], by_block[j][None, :], col_spectra)
    row_global = (PRIOR + row_ids)[:, None]
    col_global = PRIOR + col_ids
    row_points = row_global // 3
    col_points = col_global // 3
    across = (row_points % GRID - col_points % GRID).astype(jnp.float32)
    height = (row_points // GRID - col_points // GRID).astype(jnp.float32)
    distance = jnp.sqrt(across * across + height * height)
    coupling = jnp.where(row_global % 3 == col_global % 3, jnp.float32(1.0), jnp.float32(cross_weight))
    amplitude = jnp.sqrt(row_spectra[:, None] * col_spectra)
    diagonal = jnp.where(row_ids[:, None] == col_ids, row_nugget[:, None], jnp.float32(0.0))
    return coupling * amplitude * jnp.exp(-decay * distance) + diagonal


def tables():
    bins = FIRST_BIN + np.arange(FREQS)
    turns = (bins[:, None] * np.arange(STEPS)[None, :] % STEPS) * (2.0 * math.pi / STEPS)
    exact = np.concatenate([np.cos(turns), -np.sin(turns)], axis=0).astype(np.float32)
    high = exact.astype(jnp.bfloat16)
    low = (exact - high.astype(np.float32)).astype(jnp.bfloat16)
    return jnp.asarray(np.concatenate([high, high, low], axis=0))


CHIP_AXES = ("row", "y")


def exchange(x):
    return lax.all_to_all(x, CHIP_AXES, split_axis=0, concat_axis=0, tiled=True)


def swap(x):
    return lax.ppermute(x, "core", [(0, 1), (1, 0)])


def shards(prior_factor, prior_seeds, window_seeds, spectra, nugget, decay):
    cols = prior_factor[0]
    depth = cols.shape[0]
    core = lax.axis_index("core")
    chip = lax.axis_index(CHIP_AXES)
    owner = lax.axis_index(("row", "y", "core"))
    where = jnp.stack([core, owner]).astype(jnp.int32)

    with jax.named_scope("schur"):
        turned = pltpu.VMEM((WINDOW, depth), jnp.bfloat16)
        keep, send = call(
            schur_kernel,
            "schur",
            (f32(CHIPS, CHUNK, BLK),) * 2,
            [SMEM, VMEM],
            [turned],
            flops=10**9,
            moved=4 * 2**20,
        )(where, cols)
        received = swap(send)
    with jax.named_scope("reduce"):
        summed, seeds = lax.optimization_barrier((keep + received, prior_seeds[0]))
        parts = exchange(summed)
    with jax.named_scope("prior"):
        yield_keep, yield_send = call(
            prior_kernel,
            "prior",
            (f32(WINDOW // 2, 2 * SEEDS),) * 2,
            [SMEM, VMEM, VMEM],
            [turned],
            flops=1000,
            moved=1000,
        )(where, cols, seeds)
    with jax.named_scope("known"):
        known = coherence_chunk(spectra[0], nugget[0], decay[0], core, chip)
        known, yield_keep, yield_send = lax.optimization_barrier((known, yield_keep, yield_send))
        yield_received = swap(yield_send)
        chunk = known - jnp.sum(parts, axis=0)
        chunk, yield_keep, window_index = lax.optimization_barrier((chunk, yield_keep, window_seeds[0]))
        prior = yield_keep + yield_received
    with jax.named_scope("gather"):
        own = exchange(jnp.broadcast_to(chunk[None], (CHIPS, CHUNK, BLK)))
    with jax.named_scope("window"):
        high, low = call(
            window_waves_kernel,
            "window_waves",
            (jax.ShapeDtypeStruct((2 * SEEDS, WINDOW), jnp.bfloat16),) * 2,
            [VMEM],
            flops=1000,
            moved=1000,
        )(window_index.T)
        own, prior, high, low = lax.optimization_barrier((own, prior, high, low))
        other = swap(own)
        prior_parts = exchange(prior.reshape(CHIPS, 32, 2 * SEEDS))
    with jax.named_scope("factor"):
        square = pltpu.VMEM((WINDOW, WINDOW), jnp.float32)
        waves = pltpu.VMEM((2 * SEEDS, WINDOW), jnp.bfloat16)
        amp = call(
            factor_kernel,
            "factor",
            f32(FREQS, 32, BLK),
            [SMEM] + [VMEM] * 2 + [HBM] * 2,
            [square, square, pltpu.VMEM((8, BLK, BLK), jnp.float32), waves, waves, pltpu.SemaphoreType.DMA((2,))],
            flops=60 * 10**9,
            moved=4 * 2**20,
            vmem=VMEM_LAST,
        )(where, own, other, high, low)
    with jax.named_scope("amplitude"):
        amp = call(
            finish_kernel,
            "finish",
            f32(FREQS, 32, BLK),
            [VMEM, VMEM],
            [pltpu.VMEM((FREQS, 32, BLK), jnp.float32)],
            flops=10**8,
            moved=2 * 2**20,
        )(amp, prior_parts)
        amp = lax.all_to_all(amp, "freq", split_axis=0, concat_axis=0, tiled=True)
    with jax.named_scope("synthesis"):
        series = pl.pallas_call(
            synthesis_kernel,
            grid=(2,),
            out_shape=f32(4, 16, 32, STEPS),
            in_specs=[
                pl.BlockSpec((FREQS, 2, 8, BLK), lambda i: (0, 0, i, 0)),
                pl.BlockSpec((6 * FREQS, STEPS), lambda i: (0, 0)),
            ],
            out_specs=pl.BlockSpec((4, 8, 32, STEPS), lambda i: (0, i, 0, 0)),
            compiler_params=pltpu.CompilerParams(vmem_limit_bytes=VMEM_BYTES),
            cost_estimate=pl.CostEstimate(flops=10**8, bytes_accessed=2 * 2**20, transcendentals=0),
            name="synthesis",
        )(amp.reshape(FREQS, 2, 16, BLK), tables())
        return series.reshape(64, 32, STEPS)


def solution(mesh):
    chips = Mesh(mesh.devices.reshape(8, 4, 4, 2), ("freq", "row", "y", "core"))
    own = ("row", "y", "core")
    in_specs = (
        P("freq", own, None),
        P("freq", own, None),
        P("freq", None, None),
        P("freq", None),
        P("freq", None),
        P("freq"),
    )
    return jax.shard_map(shards, mesh=chips, in_specs=in_specs, out_specs=P("freq", own, None), check_vma=False)
```
